256 devices in a mesh: ctx: 64 (over z, x, core), head: 4 (over y).
Axes of the slice: x: 4, y: 4, z: 8, core: 2. Of those that a mesh axis runs over, the one named last changes fastest.
Arguments:
- query_states: bfloat16 [32768, 2048], P('ctx', 'head'), may hold values from -6 to 6
- key_states: bfloat16 [32768, 256], P('ctx'), may hold values from -6 to 6
- value_states: bfloat16 [32768, 256], P('ctx'), may hold values from -6 to 6
- out_grad: bfloat16 [32768, 2048], P('ctx', 'head'), may hold values from -6 to 6
- lengths: int32 [64], replicated, may hold values from 1 to 2048, as said below
Outputs:
- attended: bfloat16 [32768, 2048], P('ctx', 'head')
- query_grad: bfloat16 [32768, 2048], P('ctx', 'head')
- key_grad: bfloat16 [32768, 256], P('ctx', 'head')
- value_grad: bfloat16 [32768, 256], P('ctx', 'head')
The draws below stay inside these ranges and needn't reach their ends.
Inputs may be any that keep to these rules, and one draw needn't show every extreme that they name: The lengths sum to 32768; the first document has 256 tokens and the second exactly 2048.
All inputs are finite; a program needn't handle non-finite values.
Results may differ from the reference program's by a relative error of at most 0.028.
Values may be sent and summed in bfloat16 or wider, within the bound.
No kernel may reach another device: no remote copies, remote signals or barrier semaphores. Data moves between devices by JAX's collectives and lax.ppermute only.
A program may use at most 128 MiB of HBM per device.

```python
import jax
import jax.numpy as jnp
from jax import lax

HEAD_DIM = 128
HEADS = 16
KV_HEADS = 2
WINDOW = 4
TOK_DEV = 512
TOKENS = 32768
DOCMAX = 2048
NDOCS = 64
N_CTX = 64


def draw_query_states(key, part):
    key = jax.random.fold_in(key, 11)
    result = jax.random.truncated_normal(key, -6.0, 6.0, (TOKENS, HEADS * HEAD_DIM))
    return result.astype(jnp.bfloat16)


def draw_key_states(key, part):
    key = jax.random.fold_in(key, 23)
    result = jax.random.truncated_normal(key, -6.0, 6.0, (TOKENS, KV_HEADS * HEAD_DIM))
    return result.astype(jnp.bfloat16)


def draw_lengths(key, part):
    key = jax.random.fold_in(key, 37)
    others = NDOCS - 2
    rest = TOKENS - TOK_DEV // 2 - DOCMAX
    levels = jax.random.randint(key, (others,), 0, 3)
    weight = jnp.power(2, levels).astype(jnp.int32)
    total_weight = jnp.sum(weight)
    base = 1 + weight * (rest - others) // total_weight
    remainder = rest - jnp.sum(base)
    base = base + (jnp.arange(others, dtype=jnp.int32) < remainder).astype(jnp.int32)
    leading = jnp.array([TOK_DEV // 2, DOCMAX], jnp.int32)
    return jnp.concatenate([leading, base.astype(jnp.int32)]).astype(jnp.int32)


def level_of(key, extent, shards, smallest, largest):
    level, own = 1.0, jax.random.fold_in(key, 6)
    for dim, shards_of in shards:
        draws = jnp.exp(jax.random.uniform(jax.random.fold_in(own, dim), (shards_of,), jnp.float32, smallest / len(shards), largest / len(shards)))
        level = level * jnp.repeat(draws, extent[dim] // shards_of).reshape([-1 if axis == dim else 1 for axis in range(len(extent))])
    return level


def gaussian(rng, shape, deviation, limit, pieces=(), kind=jnp.bfloat16):
    entries = jax.random.normal(rng, shape, jnp.float32) * deviation
    if len(pieces) > 0:
        entries = level_of(rng, shape, pieces, -0.22, 0.18) * entries
    return jnp.clip(entries, min=-limit, max=limit).astype(kind)


def setup_inputs(seed: int = 0) -> dict:
    key_list = jax.random.split(jax.random.key(seed), 6)
    return {
        "query_states": draw_query_states(jax.random.fold_in(key_list[5], 71), 0),
        "key_states": draw_key_states(jax.random.fold_in(key_list[5], 71), 0),
        "value_states": gaussian(key_list[2], (TOKENS, KV_HEADS * HEAD_DIM), 1.0, 6.0, ((0, 64),)),
        "out_grad": gaussian(key_list[3], (TOKENS, HEADS * HEAD_DIM), 1.0, 6.0, ((0, 64), (1, 4))),
        "lengths": draw_lengths(jax.random.fold_in(key_list[5], 71), 0),
    }


def segment_ids(lengths, positions):
    doc_ends = jnp.cumsum(lengths).astype(jnp.int32)
    return jnp.sum((doc_ends[None, :] <= positions[:, None]).astype(jnp.int32), axis=1).astype(jnp.int32)


def reference(query_states, key_states, value_states, out_grad, lengths):
    score_scale = HEAD_DIM ** -0.5
    group_size = HEADS // KV_HEADS
    kv_width = KV_HEADS * HEAD_DIM
    span = (WINDOW + 1) * TOK_DEV
    lead = WINDOW * TOK_DEV
    positions = jnp.arange(TOKENS, dtype=jnp.int32)
    segment = segment_ids(lengths, positions)
    padded_keys = jnp.concatenate([jnp.zeros((lead, kv_width), key_states.dtype), key_states], axis=0)
    padded_values = jnp.concatenate([jnp.zeros((lead, kv_width), value_states.dtype), value_states], axis=0)
    padded_segment = jnp.concatenate([jnp.full((lead,), -1, jnp.int32), segment])
    head_map = jnp.arange(HEADS, dtype=jnp.int32) // group_size

    def one_block(block_index):
        row_start = (block_index * TOK_DEV).astype(jnp.int32)
        query_block = lax.dynamic_slice_in_dim(query_states, row_start, TOK_DEV, 0).astype(jnp.float32).reshape(TOK_DEV, HEADS, HEAD_DIM)
        grad_block = lax.dynamic_slice_in_dim(out_grad, row_start, TOK_DEV, 0).astype(jnp.float32).reshape(TOK_DEV, HEADS, HEAD_DIM)
        key_block = lax.dynamic_slice_in_dim(padded_keys, row_start, span, 0).astype(jnp.float32).reshape(span, KV_HEADS, HEAD_DIM)[:, head_map]
        value_block = lax.dynamic_slice_in_dim(padded_values, row_start, span, 0).astype(jnp.float32).reshape(span, KV_HEADS, HEAD_DIM)[:, head_map]
        query_seg = lax.dynamic_slice_in_dim(segment, row_start, TOK_DEV, 0)
        key_seg = lax.dynamic_slice_in_dim(padded_segment, row_start, span, 0)
        query_pos = row_start + jnp.arange(TOK_DEV, dtype=jnp.int32)
        key_pos = row_start - lead + jnp.arange(span, dtype=jnp.int32)
        allowed = (query_seg[:, None] == key_seg[None, :]) & (key_pos[None, :] <= query_pos[:, None])
        scores = jnp.einsum("thd,shd->hts", query_block, key_block) * score_scale
        scores = jnp.where(allowed[None], scores, -jnp.inf)
        row_max = jnp.max(scores, axis=2, keepdims=True)
        weights = jnp.exp(scores - row_max)
        row_total = jnp.sum(weights, axis=2, keepdims=True)
        weights = weights / row_total
        prob_rounded = lax.optimization_barrier(weights.astype(jnp.bfloat16)).astype(jnp.float32)
        attended = jnp.einsum("hts,shd->thd", prob_rounded, value_block).astype(jnp.bfloat16)
        grad_dot = jnp.sum(grad_block * attended.astype(jnp.float32), axis=2).T[:, :, None]
        prob_grad = jnp.einsum("thd,shd->hts", grad_block, value_block)
        score_grad = lax.optimization_barrier((weights * (prob_grad - grad_dot)).astype(jnp.bfloat16)).astype(jnp.float32)
        query_grad = (jnp.einsum("hts,shd->thd", score_grad, key_block) * score_scale).astype(jnp.bfloat16)
        key_terms = (jnp.einsum("hts,thd->shd", score_grad, query_block) * score_scale).reshape(span, KV_HEADS, group_size, HEAD_DIM).sum(axis=2)
        value_terms = jnp.einsum("hts,thd->shd", prob_rounded, grad_block).reshape(span, KV_HEADS, group_size, HEAD_DIM).sum(axis=2)
        return (attended.reshape(TOK_DEV, HEADS * HEAD_DIM), query_grad.reshape(TOK_DEV, HEADS * HEAD_DIM),
                key_terms.reshape(span, kv_width), value_terms.reshape(span, kv_width))

    results = lax.map(one_block, jnp.arange(N_CTX, dtype=jnp.int32))
    attended = results[0].reshape(TOKENS, HEADS * HEAD_DIM)
    query_grad = results[1].reshape(TOKENS, HEADS * HEAD_DIM)
    extra = jnp.zeros((WINDOW, span, kv_width), results[2].dtype)
    key_pieces = jnp.concatenate([results[2], extra], axis=0)
    value_pieces = jnp.concatenate([results[3], extra], axis=0)
    key_grad = jnp.zeros((N_CTX, TOK_DEV, kv_width), results[2].dtype)
    value_grad = jnp.zeros((N_CTX, TOK_DEV, kv_width), results[3].dtype)
    for distance in range(WINDOW + 1):
        offset = (WINDOW - distance) * TOK_DEV
        key_grad = key_grad + key_pieces[distance:distance + N_CTX, offset:offset + TOK_DEV]
        value_grad = value_grad + value_pieces[distance:distance + N_CTX, offset:offset + TOK_DEV]
    return (attended, query_grad, key_grad.reshape(TOKENS, kv_width).astype(jnp.bfloat16),
            value_grad.reshape(TOKENS, kv_width).astype(jnp.bfloat16))
```

```python
import math

import jax
import jax.numpy as jnp
from jax import lax
from jax.experimental import pallas as pl
from jax.experimental.pallas import tpu as pltpu
from jax.sharding import PartitionSpec as P

HEAD_DIM = 128
HEADS = 16
KV_HEADS = 2
WINDOW = 4
TOK_DEV = 512
NDOCS = 64
LOCAL = 4
TILE = 256
SPAN = (WINDOW + 1) * TOK_DEV
N_TILES = SPAN // TILE
LANES = LOCAL * TILE
SCALE = HEAD_DIM ** (-0.5)
SCALE_LOG2 = SCALE * math.log2(math.e)
NEG = -1e30


def contract_last(first_matrix, second_matrix):
    return lax.dot_general(
        first_matrix, second_matrix, (((1,), (1,)), ((), ())), preferred_element_type=jnp.float32
    )


def matmul(first_matrix, second_matrix):
    return jnp.dot(first_matrix, second_matrix, preferred_element_type=jnp.float32)


def attention_kernel(
    lengths_ref, block_ref, q_ref, grad_ref, kv0, kv1, kv2, kv3, kv4,
    out_ref, dq_ref, t0, t1, t2, t3, t4,
    kv_buf, scores, kv_acc, q_cat, g_cat, o_acc, dq_acc, sems,
):
    copies = []
    for distance, kv in enumerate((kv0, kv1, kv2, kv3, kv4)):
        row = (WINDOW - distance) * TOK_DEV
        copy = pltpu.make_async_copy(kv, kv_buf.at[pl.ds(row, TOK_DEV)], sems.at[distance])
        copy.start()
        copies.append(copy)
    kv_acc[...] = jnp.zeros_like(kv_acc)
    first_query = block_ref[0] * TOK_DEV
    origin = first_query - WINDOW * TOK_DEV
    lane_pos = first_query + lax.broadcasted_iota(jnp.int32, (1, TOK_DEV), 1)

    def next_doc(doc, carry):
        end, lane_start, edges = carry
        end = end + lengths_ref[doc]
        lane_start = jnp.where(lane_pos >= end, end, lane_start)
        edges = tuple(
            jnp.where(first_query + place >= end, end, edge)
            for place, edge in zip((0, TILE - 1, TILE, TOK_DEV - 1), edges)
        )
        return end, lane_start, edges

    zero = jnp.int32(0)
    _, lane_start, edges = lax.fori_loop(
        0, NDOCS, next_doc, (zero, jnp.zeros((1, TOK_DEV), jnp.int32), (zero,) * 4), unroll=8
    )
    for copy in copies:
        copy.wait()

    for half in range(TOK_DEV // TILE):
        rows = slice(half * TILE, (half + 1) * TILE)
        for head in range(LOCAL):
            cols = slice(head * HEAD_DIM, (head + 1) * HEAD_DIM)
            place = slice(head * TILE, (head + 1) * TILE)
            q_cat[place, :] = q_ref[rows, cols]
            g_cat[place, :] = grad_ref[rows, cols]
        diagonal = WINDOW * TOK_DEV // TILE + half
        start_rel = jnp.concatenate([lane_start[:, rows] - origin] * LOCAL, axis=1)
        query_rel = jnp.concatenate([lane_pos[:, rows] - origin] * LOCAL, axis=1)
        lowest = lax.div(edges[2 * half] - origin, TILE)
        first_full = jnp.minimum(
            lax.div(edges[2 * half + 1] - origin + TILE - 1, TILE), diagonal
        )
        o_acc[...] = jnp.zeros_like(o_acc)

        def forward_tile(masked, tile, carry):
            row_max, total = carry
            kv_rows = pl.ds(pl.multiple_of(tile * TILE, TILE), TILE)
            keys = kv_buf[kv_rows, :HEAD_DIM]
            values = kv_buf[kv_rows, HEAD_DIM:]
            raw = contract_last(keys, q_cat[...])
            if masked:
                key_rel = tile * TILE + lax.broadcasted_iota(jnp.int32, (TILE, LANES), 0)
                raw = jnp.where((key_rel >= start_rel) & (key_rel <= query_rel), raw, NEG)
            scores[tile] = raw
            new_max = jnp.maximum(row_max, jnp.max(raw, axis=0, keepdims=True))
            weights = jnp.exp2((raw - new_max) * SCALE_LOG2)
            fade = jnp.exp2((row_max - new_max) * SCALE_LOG2)
            total = total * fade + jnp.sum(weights, axis=0, keepdims=True)
            o_acc[...] = o_acc[...] * fade + matmul(values.T, weights.astype(jnp.bfloat16))
            return new_max, total

        def forward_masked(tile, carry):
            return forward_tile(True, tile, carry)

        def forward_full(tile, carry):
            return forward_tile(False, tile, carry)

        carry = (jnp.full((1, LANES), NEG, jnp.float32), jnp.zeros((1, LANES), jnp.float32))
        carry = forward_masked(diagonal, carry)
        carry = lax.fori_loop(first_full, diagonal, forward_full, carry)
        carry = lax.fori_loop(lowest, first_full, forward_masked, carry)
        row_max, total = carry
        attended = (o_acc[...] * (1.0 / total)).astype(jnp.bfloat16).astype(jnp.float32)
        grad_dots = []
        for head in range(LOCAL):
            cols = slice(head * HEAD_DIM, (head + 1) * HEAD_DIM)
            place = slice(head * TILE, (head + 1) * TILE)
            att_head = attended[:, place].T
            out_ref[rows, cols] = att_head.astype(jnp.bfloat16)
            grad_t = grad_ref[rows, cols].astype(jnp.float32).T
            grad_dots.append(jnp.sum(grad_t * attended[:, place], axis=0, keepdims=True))
        grad_dot = jnp.concatenate(grad_dots, axis=1)
        log_total = row_max * SCALE_LOG2 + jnp.log2(total)
        dq_acc[...] = jnp.zeros_like(dq_acc)

        def backward_tile(tile, carry):
            kv_rows = pl.ds(pl.multiple_of(tile * TILE, TILE), TILE)
            keys = kv_buf[kv_rows, :HEAD_DIM]
            values = kv_buf[kv_rows, HEAD_DIM:]
            weights = jnp.exp2(scores[tile] * SCALE_LOG2 - log_total)
            prob_grad = contract_last(values, g_cat[...])
            score_grad = (weights * (prob_grad - grad_dot)).astype(jnp.bfloat16)
            prob = weights.astype(jnp.bfloat16)
            kv_acc[kv_rows, HEAD_DIM:] += matmul(prob, g_cat[...])
            kv_acc[kv_rows, :HEAD_DIM] += matmul(score_grad, q_cat[...])
            dq_acc[...] += matmul(keys.T, score_grad)
            return carry

        lax.fori_loop(lowest, diagonal + 1, backward_tile, 0)
        for head in range(LOCAL):
            cols = slice(head * HEAD_DIM, (head + 1) * HEAD_DIM)
            place = slice(head * TILE, (head + 1) * TILE)
            dq_ref[rows, cols] = (dq_acc[:, place].T * SCALE).astype(jnp.bfloat16)
    for distance, term in enumerate((t0, t1, t2, t3, t4)):
        row = (WINDOW - distance) * TOK_DEV
        term[:, :HEAD_DIM] = (kv_acc[row : row + TOK_DEV, :HEAD_DIM] * SCALE).astype(term.dtype)
        term[:, HEAD_DIM:] = kv_acc[row : row + TOK_DEV, HEAD_DIM:].astype(term.dtype)


def attention_block(lengths, block, queries, grads, kv_blocks):
    vmem = pl.BlockSpec(memory_space=pltpu.VMEM)
    smem = pl.BlockSpec(memory_space=pltpu.SMEM)
    anywhere = pl.BlockSpec(memory_space=pl.ANY)
    wide = jax.ShapeDtypeStruct((TOK_DEV, LOCAL * HEAD_DIM), jnp.bfloat16)
    term = jax.ShapeDtypeStruct((TOK_DEV, 2 * HEAD_DIM), jnp.bfloat16)
    own = jax.ShapeDtypeStruct((TOK_DEV, 2 * HEAD_DIM), jnp.float32)
    return pl.pallas_call(
        attention_kernel,
        out_shape=[wide, wide, own, term, term, term, term],
        in_specs=[smem, smem, vmem, vmem] + [anywhere] * 5,
        out_specs=[vmem] * 7,
        scratch_shapes=[
            pltpu.VMEM((SPAN, 2 * HEAD_DIM), jnp.bfloat16),
            pltpu.VMEM((N_TILES, TILE, LANES), jnp.float32),
            pltpu.VMEM((SPAN, 2 * HEAD_DIM), jnp.float32),
            pltpu.VMEM((LANES, HEAD_DIM), jnp.bfloat16),
            pltpu.VMEM((LANES, HEAD_DIM), jnp.bfloat16),
            pltpu.VMEM((HEAD_DIM, LANES), jnp.float32),
            pltpu.VMEM((HEAD_DIM, LANES), jnp.float32),
            pltpu.SemaphoreType.DMA((WINDOW + 1,)),
        ],
        compiler_params=pltpu.CompilerParams(vmem_limit_bytes=40 * 1024 * 1024),
        cost_estimate=pl.CostEstimate(
            flops=5 * 10**9, bytes_accessed=4 * 10**6, transcendentals=6 * 10**6
        ),
        name="attention",
    )(lengths, block, queries, grads, *kv_blocks)


def passed_along(value, axis, steps):
    count = lax.axis_size(axis)
    initial, last = (max(0, -steps), min(count, count - steps))
    return lax.ppermute(value, axis, [(source, source + steps) for source in range(initial, last)])


def from_partner(value, axis, apart):
    mask = 2**apart
    pairs = [(source, source ^ mask) for source in range(lax.axis_size(axis))]
    return lax.ppermute(value, axis, pairs)


def column_half(matrix, which, half_width):
    return lax.dynamic_slice_in_dim(matrix, which * half_width, half_width, 1)


def shards(query_states, key_states, value_states, out_grad, lengths):
    half_width = HEAD_DIM // 2
    block_index = lax.axis_index("ctx")
    head_index = lax.axis_index("head")
    kv_start = head_index * LOCAL // (HEADS // KV_HEADS) * HEAD_DIM
    own_half = head_index % 2
    other_half = 1 - own_half
    own_keys = lax.dynamic_slice_in_dim(key_states, kv_start, HEAD_DIM, 1)
    own_values = lax.dynamic_slice_in_dim(value_states, kv_start, HEAD_DIM, 1)
    own_pair = jnp.concatenate([own_keys, own_values], axis=1)
    blocks = [own_pair]
    for distance in range(1, WINDOW + 1):
        blocks.append(passed_along(own_pair, "ctx", distance))
    attended, query_grad, *terms = attention_block(
        lengths, block_index.astype(jnp.int32).reshape(1), query_states, out_grad, blocks
    )
    gathered = terms[0]
    for distance in range(1, WINDOW + 1):
        gathered = gathered + passed_along(terms[distance], "ctx", -distance).astype(jnp.float32)
    key_sum = gathered[:, :HEAD_DIM]
    value_sum = gathered[:, HEAD_DIM:]
    outgoing = jnp.concatenate(
        [
            column_half(key_sum, other_half, half_width),
            column_half(value_sum, other_half, half_width),
        ],
        axis=1,
    )
    received = from_partner(outgoing.astype(jnp.bfloat16), "head", 0).astype(jnp.float32)
    key_part = column_half(key_sum, own_half, half_width) + received[:, :half_width]
    value_part = column_half(value_sum, own_half, half_width) + received[:, half_width:]
    return attended, query_grad, key_part.astype(jnp.bfloat16), value_part.astype(jnp.bfloat16)


def solution(mesh):
    return jax.shard_map(
        shards,
        mesh=mesh,
        in_specs=(P("ctx", "head"), P("ctx", None), P("ctx", None), P("ctx", "head"), P()),
        out_specs=(P("ctx", "head"), P("ctx", "head"), P("ctx", "head"), P("ctx", "head")),
        check_vma=False,
    )
```

```python
import math

import jax
import jax.numpy as jnp
from jax import lax
from jax.experimental import pallas as pl
from jax.experimental.pallas import tpu as pltpu
from jax.sharding import PartitionSpec as P

HEAD_DIM = 128
HEADS = 16
KV_HEADS = 2
WINDOW = 4
TOK_DEV = 512
NDOCS = 64
LOCAL = 4
HALF = HEAD_DIM // 2
TILE = 256
SPAN = (WINDOW + 1) * TOK_DEV
N_TILES = SPAN // TILE
LANES = LOCAL * TILE
SCALE = HEAD_DIM ** (-0.5)
SCALE_LOG2 = SCALE * math.log2(math.e)
NEG = -1e30


def contract_last(first_matrix, second_matrix):
    return lax.dot_general(
        first_matrix, second_matrix, (((1,), (1,)), ((), ())), preferred_element_type=jnp.float32
    )


def matmul(first_matrix, second_matrix):
    return jnp.dot(first_matrix, second_matrix, preferred_element_type=jnp.float32)


def attention_kernel(
    lengths_ref, block_ref, q_ref, grad_ref, kv0, kv1, kv2, kv3, kv4, far,
    out_ref, dq_ref, t0, t1, t2, t3, t4a, t4b,
    kv_buf, scores, grads, kv_acc, kv_t, q_cat, g_cat, q_t, g_t, o_acc, dq_acc, sems,
):
    is_far = block_ref[1] == 1

    def copy_in(source, row, rows, place):
        return pltpu.make_async_copy(source, kv_buf.at[pl.ds(row, rows)], sems.at[place])

    always = [
        copy_in(kv, (WINDOW - distance) * TOK_DEV, TOK_DEV, distance)
        for distance, kv in enumerate((kv0, kv1, kv2))
    ]
    near_only = [copy_in(kv3, TOK_DEV, TOK_DEV, 3), copy_in(kv4, TILE, TILE, 4)]
    far_only = [copy_in(far.at[0], TOK_DEV, TOK_DEV, 3), copy_in(far.at[1], 0, TOK_DEV, 4)]
    for copy in always:
        copy.start()

    @pl.when(is_far)
    def _():
        for copy in far_only:
            copy.start()

    @pl.when(jnp.logical_not(is_far))
    def _():
        for copy in near_only:
            copy.start()

    kv_acc[...] = jnp.zeros_like(kv_acc)
    first_query = block_ref[0] * TOK_DEV
    origin = first_query - WINDOW * TOK_DEV
    lane_pos = first_query + lax.broadcasted_iota(jnp.int32, (1, TOK_DEV), 1)

    def next_doc(doc, carry):
        end, lane_start, edges = carry
        end = end + lengths_ref[doc]
        lane_start = jnp.where(lane_pos >= end, end, lane_start)
        edges = tuple(
            jnp.where(first_query + place >= end, end, edge)
            for place, edge in zip((0, TILE - 1, TILE, TOK_DEV - 1), edges)
        )
        return end, lane_start, edges

    zero = jnp.int32(0)
    _, lane_start, edges = lax.fori_loop(
        0, NDOCS, next_doc, (zero, jnp.zeros((1, TOK_DEV), jnp.int32), (zero,) * 4), unroll=8
    )
    for copy in always:
        copy.wait()

    @pl.when(is_far)
    def _():
        for copy in far_only:
            copy.wait()

    @pl.when(jnp.logical_not(is_far))
    def _():
        for copy in near_only:
            copy.wait()

    for half in range(TOK_DEV // TILE):
        rows = slice(half * TILE, (half + 1) * TILE)
        for head in range(LOCAL):
            cols = slice(head * HEAD_DIM, (head + 1) * HEAD_DIM)
            place = slice(head * TILE, (head + 1) * TILE)
            q_cat[place, :] = q_ref[rows, cols]
            g_cat[place, :] = grad_ref[rows, cols]
            q_t[:, place] = q_ref[rows, cols].T
            g_t[:, place] = grad_ref[rows, cols].T
        diagonal = WINDOW * TOK_DEV // TILE + half
        start_rel = jnp.concatenate([lane_start[:, rows] - origin] * LOCAL, axis=1)
        query_rel = jnp.concatenate([lane_pos[:, rows] - origin] * LOCAL, axis=1)
        lowest = lax.div(edges[2 * half] - origin, TILE)
        first_full = jnp.minimum(
            lax.div(edges[2 * half + 1] - origin + TILE - 1, TILE), diagonal
        )
        def score_tile(masked, tile, row_max):
            kv_rows = pl.ds(pl.multiple_of(tile * TILE, TILE), TILE)
            raw = matmul(kv_buf[kv_rows, :HEAD_DIM], q_t[...])
            if masked:
                key_rel = tile * TILE + lax.broadcasted_iota(jnp.int32, (TILE, LANES), 0)
                raw = jnp.where((key_rel >= start_rel) & (key_rel <= query_rel), raw, NEG)
            scores[tile] = raw
            if half == 0 or masked:
                kv_t[tile] = kv_buf[kv_rows, :].T
            return jnp.maximum(row_max, jnp.max(raw.reshape(TILE // 8, 8, LANES), axis=0))

        def score_masked(tile, row_max):
            return score_tile(True, tile, row_max)

        def score_full(tile, row_max):
            return score_tile(False, tile, row_max)

        row_max = score_masked(diagonal, jnp.full((8, LANES), NEG, jnp.float32))
        row_max = lax.fori_loop(first_full, diagonal, score_full, row_max)
        row_max = lax.fori_loop(lowest, first_full, score_masked, row_max)
        shift = jnp.max(row_max, axis=0, keepdims=True) * SCALE_LOG2

        def total_tile(tile, carry):
            total, dots = carry
            kv_rows = pl.ds(pl.multiple_of(tile * TILE, TILE), TILE)
            prob_grad = matmul(kv_buf[kv_rows, HEAD_DIM:], g_t[...])
            weights = jnp.exp2(scores[tile] * SCALE_LOG2 - shift)
            scores[tile] = weights
            grads[tile] = prob_grad
            total = total + jnp.sum(weights.reshape(TILE // 8, 8, LANES), axis=0)
            dots = dots + jnp.sum((weights * prob_grad).reshape(TILE // 8, 8, LANES), axis=0)
            return total, dots

        nothing = jnp.zeros((8, LANES), jnp.float32)
        total, dots = lax.fori_loop(lowest, diagonal + 1, total_tile, (nothing, nothing))
        inverse = 1.0 / jnp.sum(total, axis=0, keepdims=True)
        grad_dot = jnp.sum(dots, axis=0, keepdims=True) * inverse
        o_acc[...] = jnp.zeros_like(o_acc)
        dq_acc[...] = jnp.zeros_like(dq_acc)

        def backward_tile(tile, carry):
            kv_rows = pl.ds(pl.multiple_of(tile * TILE, TILE), TILE)
            keys = kv_buf[kv_rows, :HEAD_DIM]
            values = kv_buf[kv_rows, HEAD_DIM:]
            weights = scores[tile] * inverse
            score_grad = (weights * (grads[tile] - grad_dot)).astype(jnp.bfloat16)
            prob = weights.astype(jnp.bfloat16)
            kv_acc[kv_rows, HEAD_DIM:] += matmul(prob, g_cat[...])
            kv_acc[kv_rows, :HEAD_DIM] += matmul(score_grad, q_cat[...])
            o_acc[...] += matmul(kv_t[tile, HEAD_DIM:], prob)
            dq_acc[...] += matmul(kv_t[tile, :HEAD_DIM], score_grad)
            return carry

        lax.fori_loop(lowest, diagonal + 1, backward_tile, 0)
        for head in range(LOCAL):
            cols = slice(head * HEAD_DIM, (head + 1) * HEAD_DIM)
            place = slice(head * TILE, (head + 1) * TILE)
            out_ref[rows, cols] = o_acc[:, place].T.astype(jnp.bfloat16)
        for head in range(LOCAL):
            cols = slice(head * HEAD_DIM, (head + 1) * HEAD_DIM)
            place = slice(head * TILE, (head + 1) * TILE)
            dq_ref[rows, cols] = (dq_acc[:, place].T * SCALE).astype(jnp.bfloat16)
    def write_term(term, row, rows):
        keys = (kv_acc[row : row + rows, :HEAD_DIM] * SCALE).T.astype(term.dtype)
        values = kv_acc[row : row + rows, HEAD_DIM:].T.astype(term.dtype)
        for half in range(2):
            part = slice(half * HALF, (half + 1) * HALF)
            term[2 * half * HALF : (2 * half + 1) * HALF, :] = keys[part]
            term[(2 * half + 1) * HALF : (2 * half + 2) * HALF, :] = values[part]

    for distance, term in enumerate((t0, t1, t2, t3)):
        write_term(term, (WINDOW - distance) * TOK_DEV, TOK_DEV)
    write_term(t4a, 0, TILE)
    write_term(t4b, TILE, TILE)


def attention_block(lengths, block, queries, grads, kv_blocks, far_blocks):
    vmem = pl.BlockSpec(memory_space=pltpu.VMEM)
    smem = pl.BlockSpec(memory_space=pltpu.SMEM)
    anywhere = pl.BlockSpec(memory_space=pl.ANY)
    wide = jax.ShapeDtypeStruct((TOK_DEV, LOCAL * HEAD_DIM), jnp.bfloat16)
    own = jax.ShapeDtypeStruct((2 * HEAD_DIM, TOK_DEV), jnp.float32)
    term = jax.ShapeDtypeStruct((2 * HEAD_DIM, TOK_DEV), jnp.bfloat16)
    short = jax.ShapeDtypeStruct((2 * HEAD_DIM, TILE), jnp.bfloat16)
    return pl.pallas_call(
        attention_kernel,
        out_shape=[wide, wide, own, term, term, term, short, short],
        in_specs=[smem, smem, vmem, vmem] + [anywhere] * 6,
        out_specs=[vmem] * 8,
        scratch_shapes=[
            pltpu.VMEM((SPAN, 2 * HEAD_DIM), jnp.bfloat16),
            pltpu.VMEM((N_TILES, TILE, LANES), jnp.float32),
            pltpu.VMEM((N_TILES, TILE, LANES), jnp.float32),
            pltpu.VMEM((SPAN, 2 * HEAD_DIM), jnp.float32),
            pltpu.VMEM((N_TILES, 2 * HEAD_DIM, TILE), jnp.bfloat16),
            pltpu.VMEM((LANES, HEAD_DIM), jnp.bfloat16),
            pltpu.VMEM((LANES, HEAD_DIM), jnp.bfloat16),
            pltpu.VMEM((HEAD_DIM, LANES), jnp.bfloat16),
            pltpu.VMEM((HEAD_DIM, LANES), jnp.bfloat16),
            pltpu.VMEM((HEAD_DIM, LANES), jnp.float32),
            pltpu.VMEM((HEAD_DIM, LANES), jnp.float32),
            pltpu.SemaphoreType.DMA((WINDOW + 1,)),
        ],
        compiler_params=pltpu.CompilerParams(vmem_limit_bytes=44 * 1024 * 1024),
        cost_estimate=pl.CostEstimate(
            flops=5 * 10**9, bytes_accessed=4 * 10**6, transcendentals=6 * 10**6
        ),
        name="attention",
    )(lengths, block, queries, grads, *kv_blocks, far_blocks)


def moved(value, pairs):
    return lax.ppermute(value, "ctx", pairs)


def from_partner(value, axis, apart):
    mask = 2**apart
    pairs = [(source, source ^ mask) for source in range(lax.axis_size(axis))]
    return lax.ppermute(value, axis, pairs)


def pairs_at(distance, count):
    return [(source, source + distance) for source in range(count - distance)]


def needed(source, target):
    return target < 5 or source >= 4


def reversed_pairs(pairs):
    return [(target, source) for source, target in pairs]


def any_far(lengths):
    ends = jnp.cumsum(lengths)
    starts = ends - lengths
    blocks_back = (ends - 1) // TOK_DEV - starts // TOK_DEV
    return jnp.any((blocks_back >= 3) & (jnp.arange(NDOCS) != 1))


def shards(query_states, key_states, value_states, out_grad, lengths):
    count = lax.axis_size("ctx")
    block_index = lax.axis_index("ctx")
    head_index = lax.axis_index("head")
    kv_start = head_index * LOCAL // (HEADS // KV_HEADS) * HEAD_DIM
    own_half = head_index % 2
    own_keys = lax.dynamic_slice_in_dim(key_states, kv_start, HEAD_DIM, 1)
    own_values = lax.dynamic_slice_in_dim(value_states, kv_start, HEAD_DIM, 1)
    own_pair = jnp.concatenate([own_keys, own_values], axis=1)
    near = {
        distance: [pair for pair in pairs_at(distance, count) if needed(*pair)]
        for distance in (1, 2)
    }
    near[3] = [(0, 3), (1, 4)]
    near[4] = [(0, 4)]
    wide = {
        distance: [pair for pair in pairs_at(distance, count) if needed(*pair)]
        for distance in (3, 4)
    }
    second = moved(own_pair, near[2])
    first = moved(own_pair, near[1])
    third = moved(own_pair, near[3])
    fourth = moved(own_pair[TILE:], near[4])
    is_far = any_far(lengths)
    far_blocks = lax.cond(
        is_far,
        lambda pair: jnp.stack([moved(pair, wide[3]), moved(pair, wide[4])]),
        lambda pair: jnp.zeros((2,) + pair.shape, pair.dtype),
        own_pair,
    )
    place = jnp.stack([block_index.astype(jnp.int32), is_far.astype(jnp.int32)])
    attended, query_grad, t0, t1, t2, t3, t4a, t4b = attention_block(
        lengths, place, query_states, out_grad, [own_pair, first, second, third, fourth], far_blocks
    )
    back4 = moved(t4b, reversed_pairs(near[4]))
    back3 = moved(t3, reversed_pairs(near[3]))
    back2 = moved(t2, reversed_pairs(near[2]))
    back1 = moved(t1, reversed_pairs(near[1]))

    def far_terms(third_term, fourth_term):
        from3 = moved(third_term, [p for p in reversed_pairs(wide[3]) if p[1] > 1])
        from4 = moved(fourth_term, [p for p in reversed_pairs(wide[4]) if p[1] > 0])
        return from3.astype(jnp.float32) + from4.astype(jnp.float32)

    far_sum = lax.cond(
        is_far,
        lambda args: far_terms(args[0], jnp.concatenate([args[1], args[2]], axis=1)),
        lambda args: jnp.zeros(t0.shape, jnp.float32),
        (t3, t4a, t4b),
    )
    sums = [back1, back2, back3, jnp.pad(back4, ((0, 0), (TILE, 0)))]
    gathered = t0 + far_sum
    for term in sums:
        gathered = gathered + term.astype(jnp.float32)
    outgoing = lax.dynamic_slice_in_dim(gathered, (1 - own_half) * HEAD_DIM, HEAD_DIM, 0)
    received = from_partner(outgoing.astype(jnp.bfloat16), "head", 0).astype(jnp.float32)
    kept = lax.dynamic_slice_in_dim(gathered, own_half * HEAD_DIM, HEAD_DIM, 0)
    both = (kept + received).astype(jnp.bfloat16)
    return attended, query_grad, both[:HALF].T, both[HALF:].T


def solution(mesh):
    return jax.shard_map(
        shards,
        mesh=mesh,
        in_specs=(P("ctx", "head"), P("ctx", None), P("ctx", None), P("ctx", "head"), P()),
        out_specs=(P("ctx", "head"), P("ctx", "head"), P("ctx", "head"), P("ctx", "head")),
        check_vma=False,
    )
```

```python
import math

import jax
import jax.numpy as jnp
from jax import lax
from jax.experimental import pallas as pl
from jax.experimental.pallas import tpu as pltpu
from jax.sharding import PartitionSpec as P

HEAD_DIM = 128
HEADS = 16
KV_HEADS = 2
WINDOW = 4
TOK_DEV = 512
NDOCS = 64
LOCAL = 4
HALF = HEAD_DIM // 2
TILE = 256
SPAN = (WINDOW + 1) * TOK_DEV
N_TILES = SPAN // TILE
LANES = LOCAL * TILE
SCALE = HEAD_DIM ** (-0.5)
SCALE_LOG2 = SCALE * math.log2(math.e)
NEG = -1e30


def contract_last(first_matrix, second_matrix):
    return lax.dot_general(
        first_matrix, second_matrix, (((1,), (1,)), ((), ())), preferred_element_type=jnp.float32
    )


def matmul(first_matrix, second_matrix):
    return jnp.dot(first_matrix, second_matrix, preferred_element_type=jnp.float32)


def attention_kernel(
    lengths_ref, block_ref, q_ref, grad_ref, kv0, kv1, kv2, swapped, kv3, kv4, far,
    out_ref, dq_ref, t0, t1, t2, t3, t4a, t4b,
    kv_buf, scores, grads, kv_acc, kv_t, q_cat, g_cat, q_t, g_t, o_acc, dq_acc, sems,
):
    block = block_ref[0]
    is_far = block_ref[1] == 1

    def copy_in(source, row, rows, place):
        return pltpu.make_async_copy(source, kv_buf.at[pl.ds(row, rows)], sems.at[place])

    by_case = (
        (block != 2, [copy_in(kv1, 3 * TOK_DEV, TOK_DEV, 1)]),
        (block == 2, [copy_in(swapped, 3 * TOK_DEV, TOK_DEV, 1)]),
        (block == 3, [copy_in(swapped, TOK_DEV, TOK_DEV, 3)]),
        (block == 4, [copy_in(kv3, TOK_DEV, TOK_DEV, 3), copy_in(kv4, TILE, TILE, 4)]),
        (
            is_far & (block > 4),
            [copy_in(far.at[0], TOK_DEV, TOK_DEV, 3), copy_in(far.at[1], 0, TOK_DEV, 4)],
        ),
    )
    always = [
        copy_in(kv0, WINDOW * TOK_DEV, TOK_DEV, 0),
        copy_in(kv2, 2 * TOK_DEV, TOK_DEV, 2),
    ]
    for copy in always:
        copy.start()
    for case, copies in by_case:

        @pl.when(case)
        def _(copies=copies):
            for copy in copies:
                copy.start()

    kv_acc[...] = jnp.zeros_like(kv_acc)
    first_query = block * TOK_DEV
    origin = first_query - WINDOW * TOK_DEV
    lane_pos = first_query + lax.broadcasted_iota(jnp.int32, (1, TOK_DEV), 1)

    def next_doc(doc, carry):
        end, lane_start, edges = carry
        end = end + lengths_ref[doc]
        lane_start = jnp.where(lane_pos >= end, end, lane_start)
        edges = tuple(
            jnp.where(first_query + place >= end, end, edge)
            for place, edge in zip((0, TILE - 1, TILE, TOK_DEV - 1), edges)
        )
        return end, lane_start, edges

    zero = jnp.int32(0)
    _, lane_start, edges = lax.fori_loop(
        0, NDOCS, next_doc, (zero, jnp.zeros((1, TOK_DEV), jnp.int32), (zero,) * 4), unroll=8
    )
    for copy in always:
        copy.wait()
    for case, copies in by_case:

        @pl.when(case)
        def _(copies=copies):
            for copy in copies:
                copy.wait()

    for half in range(TOK_DEV // TILE):
        rows = slice(half * TILE, (half + 1) * TILE)
        for head in range(LOCAL):
            cols = slice(head * HEAD_DIM, (head + 1) * HEAD_DIM)
            place = slice(head * TILE, (head + 1) * TILE)
            q_cat[place, :] = q_ref[rows, cols]
            g_cat[place, :] = grad_ref[rows, cols]
            q_t[:, place] = q_ref[rows, cols].T
            g_t[:, place] = grad_ref[rows, cols].T
        diagonal = WINDOW * TOK_DEV // TILE + half
        start_rel = jnp.concatenate([lane_start[:, rows] - origin] * LOCAL, axis=1)
        query_rel = jnp.concatenate([lane_pos[:, rows] - origin] * LOCAL, axis=1)
        lowest = lax.div(edges[2 * half] - origin, TILE)
        first_full = jnp.minimum(
            lax.div(edges[2 * half + 1] - origin + TILE - 1, TILE), diagonal
        )
        def score_tile(masked, tile, row_max):
            kv_rows = pl.ds(pl.multiple_of(tile * TILE, TILE), TILE)
            raw = matmul(kv_buf[kv_rows, :HEAD_DIM], q_t[...])
            if masked:
                key_rel = tile * TILE + lax.broadcasted_iota(jnp.int32, (TILE, LANES), 0)
                raw = jnp.where((key_rel >= start_rel) & (key_rel <= query_rel), raw, NEG)
            scores[tile] = raw
            if half == 0 or masked:
                kv_t[tile] = kv_buf[kv_rows, :].T
            return jnp.maximum(row_max, jnp.max(raw.reshape(TILE // 8, 8, LANES), axis=0))

        def score_masked(tile, row_max):
            return score_tile(True, tile, row_max)

        def score_full(tile, row_max):
            return score_tile(False, tile, row_max)

        row_max = score_masked(diagonal, jnp.full((8, LANES), NEG, jnp.float32))
        row_max = lax.fori_loop(first_full, diagonal, score_full, row_max)
        row_max = lax.fori_loop(lowest, first_full, score_masked, row_max)
        shift = jnp.max(row_max, axis=0, keepdims=True) * SCALE_LOG2

        def total_tile(tile, carry):
            total, dots = carry
            kv_rows = pl.ds(pl.multiple_of(tile * TILE, TILE), TILE)
            prob_grad = matmul(kv_buf[kv_rows, HEAD_DIM:], g_t[...])
            weights = jnp.exp2(scores[tile] * SCALE_LOG2 - shift)
            scores[tile] = weights
            grads[tile] = prob_grad
            total = total + jnp.sum(weights.reshape(TILE // 8, 8, LANES), axis=0)
            dots = dots + jnp.sum((weights * prob_grad).reshape(TILE // 8, 8, LANES), axis=0)
            return total, dots

        nothing = jnp.zeros((8, LANES), jnp.float32)
        total, dots = lax.fori_loop(lowest, diagonal + 1, total_tile, (nothing, nothing))
        inverse = 1.0 / jnp.sum(total, axis=0, keepdims=True)
        grad_dot = jnp.sum(dots, axis=0, keepdims=True) * inverse
        o_acc[...] = jnp.zeros_like(o_acc)
        dq_acc[...] = jnp.zeros_like(dq_acc)

        def backward_tile(tile, carry):
            kv_rows = pl.ds(pl.multiple_of(tile * TILE, TILE), TILE)
            keys = kv_buf[kv_rows, :HEAD_DIM]
            values = kv_buf[kv_rows, HEAD_DIM:]
            weights = scores[tile] * inverse
            score_grad = (weights * (grads[tile] - grad_dot)).astype(jnp.bfloat16)
            prob = weights.astype(jnp.bfloat16)
            kv_acc[kv_rows, HEAD_DIM:] += matmul(prob, g_cat[...])
            kv_acc[kv_rows, :HEAD_DIM] += matmul(score_grad, q_cat[...])
            o_acc[...] += matmul(kv_t[tile, HEAD_DIM:], prob)
            dq_acc[...] += matmul(kv_t[tile, :HEAD_DIM], score_grad)
            return carry

        lax.fori_loop(lowest, diagonal + 1, backward_tile, 0)
        for head in range(LOCAL):
            cols = slice(head * HEAD_DIM, (head + 1) * HEAD_DIM)
            place = slice(head * TILE, (head + 1) * TILE)
            out_ref[rows, cols] = o_acc[:, place].T.astype(jnp.bfloat16)
        for head in range(LOCAL):
            cols = slice(head * HEAD_DIM, (head + 1) * HEAD_DIM)
            place = slice(head * TILE, (head + 1) * TILE)
            dq_ref[rows, cols] = (dq_acc[:, place].T * SCALE).astype(jnp.bfloat16)
    def write_term(term, row, rows):
        keys = (kv_acc[row : row + rows, :HEAD_DIM] * SCALE).T.astype(term.dtype)
        values = kv_acc[row : row + rows, HEAD_DIM:].T.astype(term.dtype)
        for half in range(2):
            part = slice(half * HALF, (half + 1) * HALF)
            term[2 * half * HALF : (2 * half + 1) * HALF, :] = keys[part]
            term[(2 * half + 1) * HALF : (2 * half + 2) * HALF, :] = values[part]

    for distance, term in enumerate((t0, t1, t2, t3)):
        write_term(term, (WINDOW - distance) * TOK_DEV, TOK_DEV)
    write_term(t4a, 0, TILE)
    write_term(t4b, TILE, TILE)


def pick_kernel(column_ref, keys_ref, values_ref, pair_ref, high_ref, sems):
    column = pl.multiple_of(column_ref[0], HEAD_DIM)
    copies = []
    for place, source in enumerate((keys_ref, values_ref)):
        cols = pl.ds(place * HEAD_DIM, HEAD_DIM)
        copies.append(
            pltpu.make_async_copy(
                source.at[:, pl.ds(column, HEAD_DIM)], pair_ref.at[:, cols], sems.at[place]
            )
        )
        copies.append(
            pltpu.make_async_copy(
                source.at[pl.ds(TILE, TILE), pl.ds(column, HEAD_DIM)],
                high_ref.at[:, cols],
                sems.at[2 + place],
            )
        )
    for copy in copies:
        copy.start()
    for copy in copies:
        copy.wait()


def pick_block(column, keys, values):
    smem = pl.BlockSpec(memory_space=pltpu.SMEM)
    vmem = pl.BlockSpec(memory_space=pltpu.VMEM)
    anywhere = pl.BlockSpec(memory_space=pltpu.HBM)
    return pl.pallas_call(
        pick_kernel,
        out_shape=[
            jax.ShapeDtypeStruct((TOK_DEV, 2 * HEAD_DIM), jnp.bfloat16),
            jax.ShapeDtypeStruct((TILE, 2 * HEAD_DIM), jnp.bfloat16),
        ],
        in_specs=[smem, anywhere, anywhere],
        out_specs=[vmem, vmem],
        scratch_shapes=[pltpu.SemaphoreType.DMA((4,))],
        compiler_params=pltpu.CompilerParams(vmem_limit_bytes=60 * 1024 * 1024),
        cost_estimate=pl.CostEstimate(flops=0, bytes_accessed=10**6, transcendentals=0),
        name="pick",
    )(column, keys, values)


def attention_block(lengths, block, queries, grads, kv_blocks, far_blocks):
    vmem = pl.BlockSpec(memory_space=pltpu.VMEM)
    smem = pl.BlockSpec(memory_space=pltpu.SMEM)
    anywhere = pl.BlockSpec(memory_space=pl.ANY)
    wide = jax.ShapeDtypeStruct((TOK_DEV, LOCAL * HEAD_DIM), jnp.bfloat16)
    own = jax.ShapeDtypeStruct((2 * HEAD_DIM, TOK_DEV), jnp.float32)
    term = jax.ShapeDtypeStruct((2 * HEAD_DIM, TOK_DEV), jnp.bfloat16)
    short = jax.ShapeDtypeStruct((2 * HEAD_DIM, TILE), jnp.bfloat16)
    return pl.pallas_call(
        attention_kernel,
        out_shape=[wide, wide, own, term, term, term, short, short],
        in_specs=[smem, smem, vmem, vmem] + [anywhere] * 7,
        out_specs=[vmem] * 8,
        scratch_shapes=[
            pltpu.VMEM((SPAN, 2 * HEAD_DIM), jnp.bfloat16),
            pltpu.VMEM((N_TILES, TILE, LANES), jnp.float32),
            pltpu.VMEM((N_TILES, TILE, LANES), jnp.float32),
            pltpu.VMEM((SPAN, 2 * HEAD_DIM), jnp.float32),
            pltpu.VMEM((N_TILES, 2 * HEAD_DIM, TILE), jnp.bfloat16),
            pltpu.VMEM((LANES, HEAD_DIM), jnp.bfloat16),
            pltpu.VMEM((LANES, HEAD_DIM), jnp.bfloat16),
            pltpu.VMEM((HEAD_DIM, LANES), jnp.bfloat16),
            pltpu.VMEM((HEAD_DIM, LANES), jnp.bfloat16),
            pltpu.VMEM((HEAD_DIM, LANES), jnp.float32),
            pltpu.VMEM((HEAD_DIM, LANES), jnp.float32),
            pltpu.SemaphoreType.DMA((WINDOW + 1,)),
        ],
        compiler_params=pltpu.CompilerParams(vmem_limit_bytes=44 * 1024 * 1024),
        cost_estimate=pl.CostEstimate(
            flops=5 * 10**9, bytes_accessed=4 * 10**6, transcendentals=6 * 10**6
        ),
        name="attention",
    )(lengths, block, queries, grads, *kv_blocks, far_blocks)


def moved(value, pairs):
    return lax.ppermute(value, "ctx", pairs)


def from_partner(value, axis, apart):
    mask = 2**apart
    pairs = [(source, source ^ mask) for source in range(lax.axis_size(axis))]
    return lax.ppermute(value, axis, pairs)


def pairs_at(distance, count):
    return [(source, source + distance) for source in range(count - distance)]


def needed(source, target):
    return target < 5 or source >= 4


def reversed_pairs(pairs):
    return [(target, source) for source, target in pairs]


def any_far(lengths):
    ends = jnp.cumsum(lengths)
    starts = ends - lengths
    blocks_back = (ends - 1) // TOK_DEV - starts // TOK_DEV
    return jnp.any((blocks_back >= 3) & (jnp.arange(NDOCS) != 1))


def shards(query_states, key_states, value_states, out_grad, lengths):
    count = lax.axis_size("ctx")
    block_index = lax.axis_index("ctx")
    head_index = lax.axis_index("head")
    kv_start = head_index * LOCAL // (HEADS // KV_HEADS) * HEAD_DIM
    own_half = head_index % 2
    own_pair, own_high = pick_block(
        kv_start.astype(jnp.int32).reshape(1), key_states, value_states
    )
    near = {
        distance: [pair for pair in pairs_at(distance, count) if needed(*pair)]
        for distance in (1, 2)
    }
    near[3] = [(0, 3), (1, 4)]
    near[4] = [(0, 4)]
    wide = {distance: pairs_at(distance, count)[WINDOW:] for distance in (3, 4)}
    second = moved(own_pair, near[2])
    first = moved(own_pair, [pair for pair in near[1] if pair != (1, 2)])
    third = moved(own_pair, near[3][1:])
    fourth = moved(own_high, near[4])
    second, fourth, kept_pair = lax.optimization_barrier((second, fourth, own_pair))
    swapped = moved(second, [(2, 3), (3, 2)])
    is_far = any_far(lengths)
    far_blocks = lax.cond(
        is_far,
        lambda pair: jnp.stack([moved(pair, wide[3]), moved(pair, wide[4])]),
        lambda pair: jnp.zeros((2,) + pair.shape, pair.dtype),
        kept_pair,
    )
    place = jnp.stack([block_index.astype(jnp.int32), is_far.astype(jnp.int32)])
    attended, query_grad, t0, t1, t2, t3, t4a, t4b = attention_block(
        lengths, place, query_states, out_grad,
        [own_pair, first, second, swapped, third, fourth], far_blocks,
    )
    back4 = moved(t4b, reversed_pairs(near[4]))
    back3 = moved(t3, reversed_pairs(near[3]))
    back2 = moved(t2, reversed_pairs(near[2]))
    back1 = moved(t1, reversed_pairs(near[1]))
    gathered = t0 + back3.astype(jnp.float32)
    gathered = gathered + jnp.pad(back4, ((0, 0), (TILE, 0))).astype(jnp.float32)
    gathered = lax.optimization_barrier(gathered)
    gathered = gathered + back2.astype(jnp.float32) + back1.astype(jnp.float32)

    def with_far(total, third_term, low_term, high_term):
        fourth_term = jnp.concatenate([low_term, high_term], axis=1)
        from3 = moved(third_term, reversed_pairs(wide[3]))
        from4 = moved(fourth_term, reversed_pairs(wide[4]))
        return total + from3.astype(jnp.float32) + from4.astype(jnp.float32)

    gathered = lax.cond(
        is_far, with_far, lambda total, *others: total, gathered, t3, t4a, t4b
    )
    outgoing = lax.dynamic_slice_in_dim(gathered, (1 - own_half) * HEAD_DIM, HEAD_DIM, 0)
    received = from_partner(outgoing.astype(jnp.bfloat16), "head", 0).astype(jnp.float32)
    kept = lax.dynamic_slice_in_dim(gathered, own_half * HEAD_DIM, HEAD_DIM, 0)
    both = (kept + received).astype(jnp.bfloat16)
    return attended, query_grad, both[:HALF].T, both[HALF:].T


def solution(mesh):
    return jax.shard_map(
        shards,
        mesh=mesh,
        in_specs=(P("ctx", "head"), P("ctx", None), P("ctx", None), P("ctx", "head"), P()),
        out_specs=(P("ctx", "head"), P("ctx", "head"), P("ctx", "head"), P("ctx", "head")),
        check_vma=False,
    )
```

```python
import math

import jax
import jax.numpy as jnp
from jax import lax
from jax.experimental import pallas as pl
from jax.experimental.pallas import tpu as pltpu
from jax.sharding import PartitionSpec as P

HEAD_DIM = 128
HEADS = 16
KV_HEADS = 2
WINDOW = 4
TOK_DEV = 512
NDOCS = 64
LOCAL = 4
HALF = HEAD_DIM // 2
TILE = 256
SPAN = (WINDOW + 1) * TOK_DEV
HALVES = TOK_DEV // TILE
OWN_ROW = WINDOW * TOK_DEV
OWN_TILE = OWN_ROW // TILE
LANES = LOCAL * TILE
SCALE = HEAD_DIM ** (-0.5)
SCALE_LOG2 = SCALE * math.log2(math.e)
NEG = -1e30
STEP = 2


def contract_last(first_matrix, second_matrix):
    return lax.dot_general(
        first_matrix, second_matrix, (((1,), (1,)), ((), ())), preferred_element_type=jnp.float32
    )


def matmul(first_matrix, second_matrix):
    return jnp.dot(first_matrix, second_matrix, preferred_element_type=jnp.float32)


def tile_rows(tile, count):
    return pl.ds(pl.multiple_of(tile * TILE, TILE), count * TILE)


def by_sublane(array):
    return array.reshape(array.shape[0] // 8, 8, LANES)


def prepare_kernel(
    lengths_ref, block_ref, q_ref, grad_ref, pair_ref,
    bounds_ref, far_ref, start_ref, max_ref, q_cat, g_cat, q_t, g_t, own_scores, own_grads, own_t,
):
    first_query = block_ref[0] * TOK_DEV
    origin = first_query - WINDOW * TOK_DEV
    lane_pos = first_query + lax.broadcasted_iota(jnp.int32, (1, TOK_DEV), 1)

    def next_doc(doc, carry):
        start, is_far, lane_start, edges = carry
        end = start + lengths_ref[doc]
        reach = lax.div(end - 1, TOK_DEV) - lax.div(start, TOK_DEV)
        is_far = jnp.where((reach >= 3) & (doc != 1), 1, is_far)
        lane_start = jnp.where(lane_pos >= end, end, lane_start)
        edges = tuple(
            jnp.where(first_query + place >= end, end, edge)
            for place, edge in zip((0, TILE - 1, TILE, TOK_DEV - 1), edges)
        )
        return end, is_far, lane_start, edges

    zero = jnp.int32(0)
    _, is_far, lane_start, edges = lax.fori_loop(
        0, NDOCS, next_doc, (zero, zero, jnp.zeros((1, TOK_DEV), jnp.int32), (zero,) * 4), unroll=8
    )
    far_ref[0] = is_far
    start_ref[...] = lane_start - origin
    for half in range(HALVES):
        lowest = lax.div(edges[2 * half] - origin, TILE)
        full = lax.div(edges[2 * half + 1] - origin + TILE - 1, TILE)
        bounds_ref[2 * half] = jnp.minimum(lowest, OWN_TILE)
        bounds_ref[2 * half + 1] = jnp.minimum(full, OWN_TILE)
    for part in range(HALVES):
        own_t[part] = pair_ref[part * TILE : (part + 1) * TILE, :].T
    for half in range(HALVES):
        rows = slice(half * TILE, (half + 1) * TILE)
        lanes = slice(half * LANES, (half + 1) * LANES)
        for head in range(LOCAL):
            cols = slice(head * HEAD_DIM, (head + 1) * HEAD_DIM)
            place = slice(half * LANES + head * TILE, half * LANES + (head + 1) * TILE)
            q_cat[place, :] = q_ref[rows, cols]
            g_cat[place, :] = grad_ref[rows, cols]
            q_t[:, place] = q_ref[rows, cols].T
            g_t[:, place] = grad_ref[rows, cols].T
        start_rel = jnp.concatenate([lane_start[:, rows] - first_query] * LOCAL, axis=1)
        query_rel = jnp.concatenate([lane_pos[:, rows] - first_query] * LOCAL, axis=1)
        count = 1 + half
        own_rows = slice(half * TILE, (half + count) * TILE)
        keys = pair_ref[: count * TILE, :HEAD_DIM]
        values = pair_ref[: count * TILE, HEAD_DIM:]
        raw = matmul(keys, q_t[:, lanes])
        key_rel = lax.broadcasted_iota(jnp.int32, raw.shape, 0)
        raw = jnp.where((key_rel >= start_rel) & (key_rel <= query_rel), raw, NEG)
        own_scores[own_rows] = raw
        max_ref[half * 8 : (half + 1) * 8] = jnp.max(by_sublane(raw), axis=0)
        own_grads[own_rows] = matmul(values, g_t[:, lanes])


def attention_kernel(
    bounds_ref, start_ref, max_ref, q_cat, g_cat, q_t, g_t, own_scores, own_grads, own_t,
    pair_ref, kv2_ref, kv13_ref, kv4_ref,
    out_ref, dq_ref, t0, t1, t2, t3, t4a, t4b,
    kv_buf, kv_t, scores, grads, kv_acc, o_acc, dq_acc,
):
    kv_acc[...] = jnp.zeros_like(kv_acc)
    sources = (
        (1, kv13_ref, 0), (2, kv2_ref, 0), (3, kv13_ref, TOK_DEV), (4, kv4_ref, 0)
    )
    for distance, source, row in sources:
        place = (WINDOW - distance) * TOK_DEV

        @pl.when(bounds_ref[0] < OWN_TILE - 2 * (distance - 1))
        def _(source=source, row=row, place=place):
            kv_buf[place : place + TOK_DEV, :] = source[row : row + TOK_DEV, :]
            for part in range(HALVES):
                piece = source[row + part * TILE : row + (part + 1) * TILE, :]
                kv_t[place // TILE + part] = piece.T

    def in_steps(low, step, carry):
        middle = low + (OWN_TILE - low) // STEP * STEP
        carry = lax.fori_loop(
            0, (OWN_TILE - low) // STEP, lambda at, held: step(low + at * STEP, STEP, held), carry
        )
        return lax.fori_loop(middle, OWN_TILE, lambda at, held: step(at, 1, held), carry)

    for half in range(HALVES):
        rows = slice(half * TILE, (half + 1) * TILE)
        lanes = slice(half * LANES, (half + 1) * LANES)
        lowest = bounds_ref[2 * half]
        first_full = bounds_ref[2 * half + 1]
        count = 1 + half
        own_part = slice(half * TILE, (half + count) * TILE)
        own_rows = slice(OWN_ROW, OWN_ROW + count * TILE)

        def score_masked(tile, row_max):
            kv_rows = tile_rows(tile, 1)
            raw = matmul(kv_buf[kv_rows, :HEAD_DIM], q_t[:, lanes])
            key_rel = tile * TILE + lax.broadcasted_iota(jnp.int32, raw.shape, 0)
            start_rel = jnp.concatenate([start_ref[:, rows]] * LOCAL, axis=1)
            raw = jnp.where(key_rel >= start_rel, raw, NEG)
            scores[kv_rows] = raw
            return jnp.maximum(row_max, jnp.max(by_sublane(raw), axis=0))

        def score_full(tile, count, row_max):
            kv_rows = tile_rows(tile, count)
            raw = matmul(kv_buf[kv_rows, :HEAD_DIM], q_t[:, lanes])
            scores[kv_rows] = raw
            return jnp.maximum(row_max, jnp.max(by_sublane(raw), axis=0))

        row_max = in_steps(first_full, score_full, max_ref[half * 8 : (half + 1) * 8])
        row_max = lax.fori_loop(lowest, first_full, score_masked, row_max)
        shift = jnp.max(row_max, axis=0, keepdims=True) * SCALE_LOG2

        def add_totals(carry, weights, prob_grad):
            total, dots = carry
            total = total + jnp.sum(by_sublane(weights), axis=0)
            dots = dots + jnp.sum(by_sublane(weights * prob_grad), axis=0)
            return total, dots

        def total_tile(tile, count, carry):
            kv_rows = tile_rows(tile, count)
            prob_grad = matmul(kv_buf[kv_rows, HEAD_DIM:], g_t[:, lanes])
            weights = jnp.exp2(scores[kv_rows] * SCALE_LOG2 - shift)
            scores[kv_rows] = weights
            grads[kv_rows] = prob_grad
            return add_totals(carry, weights, prob_grad)

        nothing = jnp.zeros((8, LANES), jnp.float32)
        weights = jnp.exp2(own_scores[own_part] * SCALE_LOG2 - shift)
        scores[own_rows] = weights
        carry = add_totals((nothing, nothing), weights, own_grads[own_part])
        total, dots = in_steps(lowest, total_tile, carry)
        inverse = 1.0 / jnp.sum(total, axis=0, keepdims=True)
        grad_dot = jnp.sum(dots, axis=0, keepdims=True) * inverse

        def score_grads(weights, prob_grad):
            weights = weights * inverse
            score_grad = (weights * (prob_grad - grad_dot)).astype(jnp.bfloat16)
            return weights.astype(jnp.bfloat16), score_grad

        def transposed_products(turned, prob, score_grad):
            out_add = dq_add = None
            for part, piece in enumerate(turned):
                inner = slice(part * TILE, (part + 1) * TILE)
                out_part = matmul(piece[HEAD_DIM:], prob[inner])
                dq_part = matmul(piece[:HEAD_DIM], score_grad[inner])
                out_add = out_part if part == 0 else out_add + out_part
                dq_add = dq_part if part == 0 else dq_add + dq_part
            return out_add, dq_add

        def backward_tile(tile, count, carry):
            kv_rows = tile_rows(tile, count)
            prob, score_grad = score_grads(scores[kv_rows], grads[kv_rows])
            kv_acc[kv_rows, HEAD_DIM:] += matmul(prob, g_cat[lanes])
            kv_acc[kv_rows, :HEAD_DIM] += matmul(score_grad, q_cat[lanes])
            turned = [kv_t[tile + part] for part in range(count)]
            out_add, dq_add = transposed_products(turned, prob, score_grad)
            o_acc[...] += out_add
            dq_acc[...] += dq_add
            return carry

        prob, score_grad = score_grads(scores[own_rows], own_grads[own_part])
        kv_acc[own_rows, HEAD_DIM:] += matmul(prob, g_cat[lanes])
        kv_acc[own_rows, :HEAD_DIM] += matmul(score_grad, q_cat[lanes])
        turned = [own_t[part] for part in range(count)]
        o_acc[...], dq_acc[...] = transposed_products(turned, prob, score_grad)
        in_steps(lowest, backward_tile, 0)
        for head in range(LOCAL):
            cols = slice(head * HEAD_DIM, (head + 1) * HEAD_DIM)
            place = slice(head * TILE, (head + 1) * TILE)
            out_ref[rows, cols] = o_acc[:, place].T.astype(jnp.bfloat16)
            dq_ref[rows, cols] = (dq_acc[:, place].T * SCALE).astype(jnp.bfloat16)

    def write_term(term, row, rows):
        keys = (kv_acc[row : row + rows, :HEAD_DIM] * SCALE).T.astype(term.dtype)
        values = kv_acc[row : row + rows, HEAD_DIM:].T.astype(term.dtype)
        for half in range(2):
            part = slice(half * HALF, (half + 1) * HALF)
            term[2 * half * HALF : (2 * half + 1) * HALF, :] = keys[part]
            term[(2 * half + 1) * HALF : (2 * half + 2) * HALF, :] = values[part]

    for distance, term in enumerate((t0, t1, t2, t3)):
        write_term(term, (WINDOW - distance) * TOK_DEV, TOK_DEV)
    write_term(t4a, 0, TILE)
    write_term(t4b, TILE, TILE)


def pick_kernel(column_ref, keys_ref, values_ref, pair_ref, sems):
    column = pl.multiple_of(column_ref[0], HEAD_DIM)
    copies = []
    for place, source in enumerate((keys_ref, values_ref)):
        cols = pl.ds(place * HEAD_DIM, HEAD_DIM)
        copies.append(
            pltpu.make_async_copy(
                source.at[:, pl.ds(column, HEAD_DIM)], pair_ref.at[:, cols], sems.at[place]
            )
        )
    for copy in copies:
        copy.start()
    for copy in copies:
        copy.wait()


def pick_block(column, keys, values):
    smem = pl.BlockSpec(memory_space=pltpu.SMEM)
    vmem = pl.BlockSpec(memory_space=pltpu.VMEM)
    anywhere = pl.BlockSpec(memory_space=pltpu.HBM)
    return pl.pallas_call(
        pick_kernel,
        out_shape=jax.ShapeDtypeStruct((TOK_DEV, 2 * HEAD_DIM), jnp.bfloat16),
        in_specs=[smem, anywhere, anywhere],
        out_specs=vmem,
        scratch_shapes=[pltpu.SemaphoreType.DMA((2,))],
        compiler_params=pltpu.CompilerParams(vmem_limit_bytes=60 * 1024 * 1024),
        cost_estimate=pl.CostEstimate(flops=0, bytes_accessed=10**6, transcendentals=0),
        name="pick",
    )(column, keys, values)


def prepare(lengths, block, queries, grads, pair):
    vmem = pl.BlockSpec(memory_space=pltpu.VMEM)
    smem = pl.BlockSpec(memory_space=pltpu.SMEM)
    own = jax.ShapeDtypeStruct((3 * TILE, LANES), jnp.float32)
    rows = jax.ShapeDtypeStruct((HALVES * LANES, HEAD_DIM), jnp.bfloat16)
    cols = jax.ShapeDtypeStruct((HEAD_DIM, HALVES * LANES), jnp.bfloat16)
    return pl.pallas_call(
        prepare_kernel,
        out_shape=[
            jax.ShapeDtypeStruct((2 * HALVES,), jnp.int32),
            jax.ShapeDtypeStruct((1,), jnp.int32),
            jax.ShapeDtypeStruct((1, TOK_DEV), jnp.int32),
            jax.ShapeDtypeStruct((8 * HALVES, LANES), jnp.float32),
            rows, rows, cols, cols, own, own,
            jax.ShapeDtypeStruct((HALVES, 2 * HEAD_DIM, TILE), jnp.bfloat16),
        ],
        in_specs=[smem, smem, vmem, vmem, vmem],
        out_specs=[smem, smem] + [vmem] * 9,
        compiler_params=pltpu.CompilerParams(vmem_limit_bytes=24 * 1024 * 1024),
        cost_estimate=pl.CostEstimate(
            flops=2 * 10**9, bytes_accessed=10**6, transcendentals=0
        ),
        name="prepare",
    )(lengths, block, queries, grads, pair)


def attention_block(bounds, state, kv_blocks):
    vmem = pl.BlockSpec(memory_space=pltpu.VMEM)
    smem = pl.BlockSpec(memory_space=pltpu.SMEM)
    wide = jax.ShapeDtypeStruct((TOK_DEV, LOCAL * HEAD_DIM), jnp.bfloat16)
    own = jax.ShapeDtypeStruct((2 * HEAD_DIM, TOK_DEV), jnp.float32)
    term = jax.ShapeDtypeStruct((2 * HEAD_DIM, TOK_DEV), jnp.bfloat16)
    short = jax.ShapeDtypeStruct((2 * HEAD_DIM, TILE), jnp.bfloat16)
    return pl.pallas_call(
        attention_kernel,
        out_shape=[wide, wide, own, term, term, term, short, short],
        in_specs=[smem] + [vmem] * 13,
        out_specs=[vmem] * 8,
        scratch_shapes=[
            pltpu.VMEM((WINDOW * TOK_DEV, 2 * HEAD_DIM), jnp.bfloat16),
            pltpu.VMEM((OWN_TILE, 2 * HEAD_DIM, TILE), jnp.bfloat16),
            pltpu.VMEM((SPAN, LANES), jnp.float32),
            pltpu.VMEM((WINDOW * TOK_DEV, LANES), jnp.float32),
            pltpu.VMEM((SPAN, 2 * HEAD_DIM), jnp.float32),
            pltpu.VMEM((HEAD_DIM, LANES), jnp.float32),
            pltpu.VMEM((HEAD_DIM, LANES), jnp.float32),
        ],
        compiler_params=pltpu.CompilerParams(vmem_limit_bytes=40 * 1024 * 1024),
        cost_estimate=pl.CostEstimate(
            flops=5 * 10**9, bytes_accessed=4 * 10**6, transcendentals=6 * 10**6
        ),
        name="attention",
    )(bounds, *state, *kv_blocks)


def moved(value, pairs):
    return lax.ppermute(value, "ctx", pairs)


def from_partner(value, axis, apart):
    mask = 2**apart
    pairs = [(source, source ^ mask) for source in range(lax.axis_size(axis))]
    return lax.ppermute(value, axis, pairs)


def pairs_at(distance, count):
    return [(source, source + distance) for source in range(count - distance)]


def needed(source, target):
    return target < 5 or source >= 4


def reversed_pairs(pairs):
    return [(target, source) for source, target in pairs]


def shards(query_states, key_states, value_states, out_grad, lengths):
    count = lax.axis_size("ctx")
    block_index = lax.axis_index("ctx")
    head_index = lax.axis_index("head")
    kv_start = head_index * LOCAL // (HEADS // KV_HEADS) * HEAD_DIM
    own_half = head_index % 2
    own_pair = pick_block(kv_start.astype(jnp.int32).reshape(1), key_states, value_states)
    near = {
        distance: [pair for pair in pairs_at(distance, count) if needed(*pair)]
        for distance in (1, 2)
    }
    near[3] = [(0, 3), (1, 4)]
    near[4] = [(0, 4)]
    wide = {distance: pairs_at(distance, count)[WINDOW:] for distance in (3, 4)}
    second = moved(own_pair, pairs_at(2, count))
    fourth = moved(own_pair, [(0, 4), (1, 5)])
    bounds, far_flag, *state = prepare(
        lengths, block_index.astype(jnp.int32).reshape(1), query_states, out_grad, own_pair
    )
    is_far = far_flag[0] == 1
    second, fourth = lax.optimization_barrier((second, fourth))
    fourth = lax.cond(
        is_far,
        lambda got, pair: got + moved(pair, wide[4]),
        lambda got, pair: got,
        fourth, own_pair,
    )
    is_even = block_index % 2 == 0
    outbound = jnp.concatenate(
        [jnp.where(is_even, own_pair, second), jnp.where(is_even, second, fourth)], axis=0
    )
    swapped = moved(outbound, [(place, place ^ 1) for place in range(count)])
    attended, query_grad, t0, t1, t2, t3, t4a, t4b = attention_block(
        bounds, state, [own_pair, second, swapped, fourth]
    )
    back4 = moved(t4b, reversed_pairs(near[4]))
    back3 = moved(t3, reversed_pairs(near[3]))
    back2 = moved(t2, reversed_pairs(near[2]))
    back1 = moved(t1, reversed_pairs(near[1]))
    gathered = t0 + back3.astype(jnp.float32)
    gathered = gathered + jnp.pad(back4, ((0, 0), (TILE, 0))).astype(jnp.float32)
    gathered = lax.optimization_barrier(gathered)
    gathered = gathered + back2.astype(jnp.float32) + back1.astype(jnp.float32)

    def with_far(total, third_term, low_term, high_term):
        fourth_term = jnp.concatenate([low_term, high_term], axis=1)
        from3 = moved(third_term, reversed_pairs(wide[3]))
        from4 = moved(fourth_term, reversed_pairs(wide[4]))
        return total + from3.astype(jnp.float32) + from4.astype(jnp.float32)

    gathered = lax.cond(
        is_far, with_far, lambda total, *others: total, gathered, t3, t4a, t4b
    )
    outgoing = lax.dynamic_slice_in_dim(gathered, (1 - own_half) * HEAD_DIM, HEAD_DIM, 0)
    received = from_partner(outgoing.astype(jnp.bfloat16), "head", 0).astype(jnp.float32)
    kept = lax.dynamic_slice_in_dim(gathered, own_half * HEAD_DIM, HEAD_DIM, 0)
    both = (kept + received).astype(jnp.bfloat16)
    return attended, query_grad, both[:HALF].T, both[HALF:].T


def solution(mesh):
    return jax.shard_map(
        shards,
        mesh=mesh,
        in_specs=(P("ctx", "head"), P("ctx", None), P("ctx", None), P("ctx", "head"), P()),
        out_specs=(P("ctx", "head"), P("ctx", "head"), P("ctx", "head"), P("ctx", "head")),
        check_vma=False,
    )
```

```python
import math

import jax
import jax.numpy as jnp
from jax import lax
from jax.experimental import pallas as pl
from jax.experimental.pallas import tpu as pltpu
from jax.sharding import PartitionSpec as P

HEAD_DIM = 128
HEADS = 16
KV_HEADS = 2
WINDOW = 4
TOK_DEV = 512
NDOCS = 64
LOCAL = 4
HALF = HEAD_DIM // 2
TILE = 256
SPAN = (WINDOW + 1) * TOK_DEV
HALVES = TOK_DEV // TILE
OWN_ROW = WINDOW * TOK_DEV
OWN_TILE = OWN_ROW // TILE
LANES = LOCAL * TILE
SCALE = HEAD_DIM ** (-0.5)
SCALE_LOG2 = SCALE * math.log2(math.e)
NEG = -1e30
STEP = 2


def contract_last(first_matrix, second_matrix):
    return lax.dot_general(
        first_matrix, second_matrix, (((1,), (1,)), ((), ())), preferred_element_type=jnp.float32
    )


def matmul(first_matrix, second_matrix):
    return jnp.dot(first_matrix, second_matrix, preferred_element_type=jnp.float32)


def tile_rows(tile, count):
    return pl.ds(pl.multiple_of(tile * TILE, TILE), count * TILE)


def by_sublane(array):
    return array.reshape(array.shape[0] // 8, 8, LANES)


def prepare_kernel(
    lengths_ref, block_ref, q_ref, grad_ref, pair_ref,
    bounds_ref, start_ref, max_ref, q_cat, g_cat, q_t, g_t, own_scores, own_grads, own_t,
):
    first_query = block_ref[0] * TOK_DEV
    origin = first_query - WINDOW * TOK_DEV
    lane_pos = first_query + lax.broadcasted_iota(jnp.int32, (1, TOK_DEV), 1)

    def next_doc(doc, carry):
        end, lane_start, edges = carry
        end = end + lengths_ref[doc]
        lane_start = jnp.where(lane_pos >= end, end, lane_start)
        edges = tuple(
            jnp.where(first_query + place >= end, end, edge)
            for place, edge in zip((0, TILE - 1, TILE, TOK_DEV - 1), edges)
        )
        return end, lane_start, edges

    zero = jnp.int32(0)
    _, lane_start, edges = lax.fori_loop(
        0, NDOCS, next_doc, (zero, jnp.zeros((1, TOK_DEV), jnp.int32), (zero,) * 4), unroll=8
    )
    start_ref[...] = lane_start - origin
    for half in range(HALVES):
        lowest = lax.div(edges[2 * half] - origin, TILE)
        full = lax.div(edges[2 * half + 1] - origin + TILE - 1, TILE)
        bounds_ref[2 * half] = jnp.minimum(lowest, OWN_TILE)
        bounds_ref[2 * half + 1] = jnp.minimum(full, OWN_TILE)
    for part in range(HALVES):
        own_t[part] = pair_ref[part * TILE : (part + 1) * TILE, :].T
    for half in range(HALVES):
        rows = slice(half * TILE, (half + 1) * TILE)
        lanes = slice(half * LANES, (half + 1) * LANES)
        for head in range(LOCAL):
            cols = slice(head * HEAD_DIM, (head + 1) * HEAD_DIM)
            place = slice(half * LANES + head * TILE, half * LANES + (head + 1) * TILE)
            q_cat[place, :] = q_ref[rows, cols]
            g_cat[place, :] = grad_ref[rows, cols]
            q_t[:, place] = q_ref[rows, cols].T
            g_t[:, place] = grad_ref[rows, cols].T
        start_rel = jnp.concatenate([lane_start[:, rows] - first_query] * LOCAL, axis=1)
        query_rel = jnp.concatenate([lane_pos[:, rows] - first_query] * LOCAL, axis=1)
        count = 1 + half
        own_rows = slice(half * TILE, (half + count) * TILE)
        keys = pair_ref[: count * TILE, :HEAD_DIM]
        values = pair_ref[: count * TILE, HEAD_DIM:]
        raw = matmul(keys, q_t[:, lanes])
        key_rel = lax.broadcasted_iota(jnp.int32, raw.shape, 0)
        raw = jnp.where((key_rel >= start_rel) & (key_rel <= query_rel), raw, NEG)
        own_scores[own_rows] = raw
        max_ref[half * 8 : (half + 1) * 8] = jnp.max(by_sublane(raw), axis=0)
        own_grads[own_rows] = matmul(values, g_t[:, lanes])


def attention_kernel(
    bounds_ref, start_ref, max_ref, q_cat, g_cat, q_t, g_t, own_scores, own_grads, own_t,
    pair_ref, kv2_ref, kv13_ref, kv4_ref,
    out_ref, dq_ref, t0, t1, t2, t3, t4a, t4b,
    kv_buf, kv_t, scores, grads, kv_acc, o_acc, dq_acc,
):
    kv_acc[...] = jnp.zeros_like(kv_acc)
    sources = (
        (1, kv13_ref, 0), (2, kv2_ref, 0), (3, kv13_ref, TOK_DEV), (4, kv4_ref, 0)
    )
    for distance, source, row in sources:
        place = (WINDOW - distance) * TOK_DEV

        @pl.when(bounds_ref[0] < OWN_TILE - 2 * (distance - 1))
        def _(source=source, row=row, place=place):
            kv_buf[place : place + TOK_DEV, :] = source[row : row + TOK_DEV, :]
            for part in range(HALVES):
                piece = source[row + part * TILE : row + (part + 1) * TILE, :]
                kv_t[place // TILE + part] = piece.T

    def in_steps(low, step, carry):
        middle = low + (OWN_TILE - low) // STEP * STEP
        carry = lax.fori_loop(
            0, (OWN_TILE - low) // STEP, lambda at, held: step(low + at * STEP, STEP, held), carry
        )
        return lax.fori_loop(middle, OWN_TILE, lambda at, held: step(at, 1, held), carry)

    for half in range(HALVES):
        rows = slice(half * TILE, (half + 1) * TILE)
        lanes = slice(half * LANES, (half + 1) * LANES)
        lowest = bounds_ref[2 * half]
        first_full = bounds_ref[2 * half + 1]
        count = 1 + half
        own_part = slice(half * TILE, (half + count) * TILE)
        own_rows = slice(OWN_ROW, OWN_ROW + count * TILE)

        def score_masked(tile, row_max):
            kv_rows = tile_rows(tile, 1)
            raw = matmul(kv_buf[kv_rows, :HEAD_DIM], q_t[:, lanes])
            key_rel = tile * TILE + lax.broadcasted_iota(jnp.int32, raw.shape, 0)
            start_rel = jnp.concatenate([start_ref[:, rows]] * LOCAL, axis=1)
            raw = jnp.where(key_rel >= start_rel, raw, NEG)
            scores[kv_rows] = raw
            return jnp.maximum(row_max, jnp.max(by_sublane(raw), axis=0))

        def score_full(tile, count, row_max):
            kv_rows = tile_rows(tile, count)
            raw = matmul(kv_buf[kv_rows, :HEAD_DIM], q_t[:, lanes])
            scores[kv_rows] = raw
            return jnp.maximum(row_max, jnp.max(by_sublane(raw), axis=0))

        row_max = in_steps(first_full, score_full, max_ref[half * 8 : (half + 1) * 8])
        row_max = lax.fori_loop(lowest, first_full, score_masked, row_max)
        shift = jnp.max(row_max, axis=0, keepdims=True) * SCALE_LOG2

        def add_totals(carry, weights, prob_grad):
            total, dots = carry
            total = total + jnp.sum(by_sublane(weights), axis=0)
            dots = dots + jnp.sum(by_sublane(weights * prob_grad), axis=0)
            return total, dots

        def total_tile(tile, count, carry):
            kv_rows = tile_rows(tile, count)
            prob_grad = matmul(kv_buf[kv_rows, HEAD_DIM:], g_t[:, lanes])
            weights = jnp.exp2(scores[kv_rows] * SCALE_LOG2 - shift)
            scores[kv_rows] = weights
            grads[kv_rows] = prob_grad
            return add_totals(carry, weights, prob_grad)

        nothing = jnp.zeros((8, LANES), jnp.float32)
        weights = jnp.exp2(own_scores[own_part] * SCALE_LOG2 - shift)
        scores[own_rows] = weights
        carry = add_totals((nothing, nothing), weights, own_grads[own_part])
        total, dots = in_steps(lowest, total_tile, carry)
        inverse = 1.0 / jnp.sum(total, axis=0, keepdims=True)
        grad_dot = jnp.sum(dots, axis=0, keepdims=True) * inverse

        def score_grads(weights, prob_grad):
            weights = weights * inverse
            score_grad = (weights * (prob_grad - grad_dot)).astype(jnp.bfloat16)
            return weights.astype(jnp.bfloat16), score_grad

        def transposed_products(turned, prob, score_grad):
            out_add = dq_add = None
            for part, piece in enumerate(turned):
                inner = slice(part * TILE, (part + 1) * TILE)
                out_part = matmul(piece[HEAD_DIM:], prob[inner])
                dq_part = matmul(piece[:HEAD_DIM], score_grad[inner])
                out_add = out_part if part == 0 else out_add + out_part
                dq_add = dq_part if part == 0 else dq_add + dq_part
            return out_add, dq_add

        def backward_tile(tile, count, carry):
            kv_rows = tile_rows(tile, count)
            prob, score_grad = score_grads(scores[kv_rows], grads[kv_rows])
            kv_acc[kv_rows, HEAD_DIM:] += matmul(prob, g_cat[lanes])
            kv_acc[kv_rows, :HEAD_DIM] += matmul(score_grad, q_cat[lanes])
            turned = [kv_t[tile + part] for part in range(count)]
            out_add, dq_add = transposed_products(turned, prob, score_grad)
            o_acc[...] += out_add
            dq_acc[...] += dq_add
            return carry

        prob, score_grad = score_grads(scores[own_rows], own_grads[own_part])
        kv_acc[own_rows, HEAD_DIM:] += matmul(prob, g_cat[lanes])
        kv_acc[own_rows, :HEAD_DIM] += matmul(score_grad, q_cat[lanes])
        turned = [own_t[part] for part in range(count)]
        o_acc[...], dq_acc[...] = transposed_products(turned, prob, score_grad)
        in_steps(lowest, backward_tile, 0)
        for head in range(LOCAL):
            cols = slice(head * HEAD_DIM, (head + 1) * HEAD_DIM)
            place = slice(head * TILE, (head + 1) * TILE)
            out_ref[rows, cols] = o_acc[:, place].T.astype(jnp.bfloat16)
            dq_ref[rows, cols] = (dq_acc[:, place].T * SCALE).astype(jnp.bfloat16)

    def write_term(term, row, rows):
        keys = (kv_acc[row : row + rows, :HEAD_DIM] * SCALE).T.astype(term.dtype)
        values = kv_acc[row : row + rows, HEAD_DIM:].T.astype(term.dtype)
        for half in range(2):
            part = slice(half * HALF, (half + 1) * HALF)
            term[2 * half * HALF : (2 * half + 1) * HALF, :] = keys[part]
            term[(2 * half + 1) * HALF : (2 * half + 2) * HALF, :] = values[part]

    for distance, term in enumerate((t0, t1, t2, t3)):
        write_term(term, (WINDOW - distance) * TOK_DEV, TOK_DEV)
    write_term(t4a, 0, TILE)
    write_term(t4b, TILE, TILE)


def pick_kernel(column_ref, keys_ref, values_ref, pair_ref, sems):
    column = pl.multiple_of(column_ref[0], HEAD_DIM)
    copies = []
    for place, source in enumerate((keys_ref, values_ref)):
        cols = pl.ds(place * HEAD_DIM, HEAD_DIM)
        copies.append(
            pltpu.make_async_copy(
                source.at[:, pl.ds(column, HEAD_DIM)], pair_ref.at[:, cols], sems.at[place]
            )
        )
    for copy in copies:
        copy.start()
    for copy in copies:
        copy.wait()


def pick_block(column, keys, values):
    smem = pl.BlockSpec(memory_space=pltpu.SMEM)
    vmem = pl.BlockSpec(memory_space=pltpu.VMEM)
    anywhere = pl.BlockSpec(memory_space=pltpu.HBM)
    return pl.pallas_call(
        pick_kernel,
        out_shape=jax.ShapeDtypeStruct((TOK_DEV, 2 * HEAD_DIM), jnp.bfloat16),
        in_specs=[smem, anywhere, anywhere],
        out_specs=vmem,
        scratch_shapes=[pltpu.SemaphoreType.DMA((2,))],
        compiler_params=pltpu.CompilerParams(vmem_limit_bytes=60 * 1024 * 1024),
        cost_estimate=pl.CostEstimate(flops=0, bytes_accessed=10**6, transcendentals=0),
        name="pick",
    )(column, keys, values)


def prepare(lengths, block, queries, grads, pair):
    vmem = pl.BlockSpec(memory_space=pltpu.VMEM)
    smem = pl.BlockSpec(memory_space=pltpu.SMEM)
    own = jax.ShapeDtypeStruct((3 * TILE, LANES), jnp.float32)
    rows = jax.ShapeDtypeStruct((HALVES * LANES, HEAD_DIM), jnp.bfloat16)
    cols = jax.ShapeDtypeStruct((HEAD_DIM, HALVES * LANES), jnp.bfloat16)
    return pl.pallas_call(
        prepare_kernel,
        out_shape=[
            jax.ShapeDtypeStruct((2 * HALVES,), jnp.int32),
            jax.ShapeDtypeStruct((1, TOK_DEV), jnp.int32),
            jax.ShapeDtypeStruct((8 * HALVES, LANES), jnp.float32),
            rows, rows, cols, cols, own, own,
            jax.ShapeDtypeStruct((HALVES, 2 * HEAD_DIM, TILE), jnp.bfloat16),
        ],
        in_specs=[smem, smem, vmem, vmem, vmem],
        out_specs=[smem] + [vmem] * 9,
        compiler_params=pltpu.CompilerParams(vmem_limit_bytes=24 * 1024 * 1024),
        cost_estimate=pl.CostEstimate(
            flops=2 * 10**9, bytes_accessed=10**6, transcendentals=0
        ),
        name="prepare",
    )(lengths, block, queries, grads, pair)


def attention_block(bounds, state, kv_blocks):
    vmem = pl.BlockSpec(memory_space=pltpu.VMEM)
    smem = pl.BlockSpec(memory_space=pltpu.SMEM)
    wide = jax.ShapeDtypeStruct((TOK_DEV, LOCAL * HEAD_DIM), jnp.bfloat16)
    own = jax.ShapeDtypeStruct((2 * HEAD_DIM, TOK_DEV), jnp.float32)
    term = jax.ShapeDtypeStruct((2 * HEAD_DIM, TOK_DEV), jnp.bfloat16)
    short = jax.ShapeDtypeStruct((2 * HEAD_DIM, TILE), jnp.bfloat16)
    return pl.pallas_call(
        attention_kernel,
        out_shape=[wide, wide, own, term, term, term, short, short],
        in_specs=[smem] + [vmem] * 13,
        out_specs=[vmem] * 8,
        scratch_shapes=[
            pltpu.VMEM((WINDOW * TOK_DEV, 2 * HEAD_DIM), jnp.bfloat16),
            pltpu.VMEM((OWN_TILE, 2 * HEAD_DIM, TILE), jnp.bfloat16),
            pltpu.VMEM((SPAN, LANES), jnp.float32),
            pltpu.VMEM((WINDOW * TOK_DEV, LANES), jnp.float32),
            pltpu.VMEM((SPAN, 2 * HEAD_DIM), jnp.float32),
            pltpu.VMEM((HEAD_DIM, LANES), jnp.float32),
            pltpu.VMEM((HEAD_DIM, LANES), jnp.float32),
        ],
        compiler_params=pltpu.CompilerParams(vmem_limit_bytes=40 * 1024 * 1024),
        cost_estimate=pl.CostEstimate(
            flops=5 * 10**9, bytes_accessed=4 * 10**6, transcendentals=6 * 10**6
        ),
        name="attention",
    )(bounds, *state, *kv_blocks)


def moved(value, pairs):
    return lax.ppermute(value, "ctx", pairs)


def from_partner(value, axis, apart):
    mask = 2**apart
    pairs = [(source, source ^ mask) for source in range(lax.axis_size(axis))]
    return lax.ppermute(value, axis, pairs)


def pairs_at(distance, count):
    return [(source, source + distance) for source in range(count - distance)]


def needed(source, target):
    return target < 5 or source >= 4


def reversed_pairs(pairs):
    return [(target, source) for source, target in pairs]


def any_far(lengths):
    ends = jnp.cumsum(lengths)
    starts = ends - lengths
    blocks_back = (ends - 1) // TOK_DEV - starts // TOK_DEV
    return jnp.any((blocks_back >= 3) & (jnp.arange(NDOCS) != 1))


def shards(query_states, key_states, value_states, out_grad, lengths):
    count = lax.axis_size("ctx")
    block_index = lax.axis_index("ctx")
    head_index = lax.axis_index("head")
    kv_start = head_index * LOCAL // (HEADS // KV_HEADS) * HEAD_DIM
    own_half = head_index % 2
    own_pair = pick_block(kv_start.astype(jnp.int32).reshape(1), key_states, value_states)
    near = {
        distance: [pair for pair in pairs_at(distance, count) if needed(*pair)]
        for distance in (1, 2)
    }
    near[3] = [(0, 3), (1, 4)]
    near[4] = [(0, 4)]
    wide = {distance: pairs_at(distance, count)[WINDOW:] for distance in (3, 4)}
    second = moved(own_pair, pairs_at(2, count))
    fourth = moved(own_pair, [(0, 4), (1, 5)])
    is_far = any_far(lengths)
    far_fourth = lax.cond(
        is_far,
        lambda pair: moved(pair, wide[4]),
        lambda pair: jnp.zeros_like(pair),
        own_pair,
    )
    own_pair, far_fourth = lax.optimization_barrier((own_pair, far_fourth))
    bounds, *state = prepare(
        lengths, block_index.astype(jnp.int32).reshape(1), query_states, out_grad, own_pair
    )
    second, fourth, bounds = lax.optimization_barrier((second, fourth, bounds))
    fourth = fourth + far_fourth
    is_even = block_index % 2 == 0
    outbound = jnp.concatenate(
        [jnp.where(is_even, own_pair, second), jnp.where(is_even, second, fourth)], axis=0
    )
    swapped = moved(outbound, [(place, place ^ 1) for place in range(count)])
    attended, query_grad, t0, t1, t2, t3, t4a, t4b = attention_block(
        bounds, state, [own_pair, second, swapped, fourth]
    )
    back4 = moved(t4b, reversed_pairs(near[4]))
    back3 = moved(t3, reversed_pairs(near[3]))
    back2 = moved(t2, reversed_pairs(near[2]))
    back1 = moved(t1, reversed_pairs(near[1]))
    gathered = t0 + back3.astype(jnp.float32)
    gathered = gathered + jnp.pad(back4, ((0, 0), (TILE, 0))).astype(jnp.float32)
    gathered = lax.optimization_barrier(gathered)
    gathered = gathered + back2.astype(jnp.float32) + back1.astype(jnp.float32)

    def with_far(total, third_term, low_term, high_term):
        fourth_term = jnp.concatenate([low_term, high_term], axis=1)
        from3 = moved(third_term, reversed_pairs(wide[3]))
        from4 = moved(fourth_term, reversed_pairs(wide[4]))
        return total + from3.astype(jnp.float32) + from4.astype(jnp.float32)

    gathered = lax.cond(
        is_far, with_far, lambda total, *others: total, gathered, t3, t4a, t4b
    )
    outgoing = lax.dynamic_slice_in_dim(gathered, (1 - own_half) * HEAD_DIM, HEAD_DIM, 0)
    received = from_partner(outgoing.astype(jnp.bfloat16), "head", 0).astype(jnp.float32)
    kept = lax.dynamic_slice_in_dim(gathered, own_half * HEAD_DIM, HEAD_DIM, 0)
    both = (kept + received).astype(jnp.bfloat16)
    return attended, query_grad, both[:HALF].T, both[HALF:].T


def solution(mesh):
    return jax.shard_map(
        shards,
        mesh=mesh,
        in_specs=(P("ctx", "head"), P("ctx", None), P("ctx", None), P("ctx", "head"), P()),
        out_specs=(P("ctx", "head"), P("ctx", "head"), P("ctx", "head"), P("ctx", "head")),
        check_vma=False,
    )
```

```python
import math

import jax
import jax.numpy as jnp
from jax import lax
from jax.experimental import pallas as pl
from jax.experimental.pallas import tpu as pltpu
from jax.sharding import PartitionSpec as P

HEAD_DIM = 128
HEADS = 16
KV_HEADS = 2
WINDOW = 4
TOK_DEV = 512
NDOCS = 64
LOCAL = 4
HALF = HEAD_DIM // 2
TILE = 256
SPAN = (WINDOW + 1) * TOK_DEV
HALVES = TOK_DEV // TILE
OWN_ROW = WINDOW * TOK_DEV
OWN_TILE = OWN_ROW // TILE
LANES = LOCAL * TILE
SCALE = HEAD_DIM ** (-0.5)
SCALE_LOG2 = SCALE * math.log2(math.e)
NEG = -1e30
STEPS = (5, 2, 1)


def contract_last(first_matrix, second_matrix):
    return lax.dot_general(
        first_matrix, second_matrix, (((1,), (1,)), ((), ())), preferred_element_type=jnp.float32
    )


def matmul(first_matrix, second_matrix):
    return jnp.dot(first_matrix, second_matrix, preferred_element_type=jnp.float32)


def tile_rows(tile, count):
    return pl.ds(pl.multiple_of(tile * TILE, TILE), count * TILE)


def by_sublane(array):
    return array.reshape(array.shape[0] // 8, 8, LANES)


def prepare_kernel(
    start_ref, q_ref, grad_ref, pair_ref,
    max_ref, q_cat, g_cat, q_t, g_t, own_scores, own_grads, own_t,
):
    for part in range(HALVES):
        own_t[part] = pair_ref[part * TILE : (part + 1) * TILE, :].T
    for half in range(HALVES):
        rows = slice(half * TILE, (half + 1) * TILE)
        lanes = slice(half * LANES, (half + 1) * LANES)
        for head in range(LOCAL):
            cols = slice(head * HEAD_DIM, (head + 1) * HEAD_DIM)
            place = slice(half * LANES + head * TILE, half * LANES + (head + 1) * TILE)
            q_cat[place, :] = q_ref[rows, cols]
            g_cat[place, :] = grad_ref[rows, cols]
            q_t[:, place] = q_ref[rows, cols].T
            g_t[:, place] = grad_ref[rows, cols].T
        start_rel = jnp.concatenate([start_ref[:, rows] - OWN_ROW] * LOCAL, axis=1)
        lane = lax.broadcasted_iota(jnp.int32, (1, TILE), 1)
        query_rel = jnp.concatenate([lane + half * TILE] * LOCAL, axis=1)
        count = 1 + half
        own_rows = slice(half * TILE, (half + count) * TILE)
        keys = pair_ref[: count * TILE, :HEAD_DIM]
        values = pair_ref[: count * TILE, HEAD_DIM:]
        raw = matmul(keys, q_t[:, lanes])
        key_rel = lax.broadcasted_iota(jnp.int32, raw.shape, 0)
        raw = jnp.where((key_rel >= start_rel) & (key_rel <= query_rel), raw, NEG)
        own_scores[own_rows] = raw
        max_ref[half * 8 : (half + 1) * 8] = jnp.max(by_sublane(raw), axis=0)
        own_grads[own_rows] = matmul(values, g_t[:, lanes])


def attention_kernel(
    bounds_ref, start_ref, max_ref, q_cat, g_cat, q_t, g_t, own_scores, own_grads, own_t,
    pair_ref, kv2_ref, kv13_ref, kv4_ref,
    out_ref, dq_ref, t0, t1, t2, t3, t4a, t4b,
    kv_buf, kv_t, scores, grads, kv_acc, o_acc, dq_acc,
):
    kv_acc[...] = jnp.zeros_like(kv_acc)
    sources = (
        (1, kv13_ref, 0), (2, kv2_ref, 0), (3, kv13_ref, TOK_DEV), (4, kv4_ref, 0)
    )
    for distance, source, row in sources:
        place = (WINDOW - distance) * TOK_DEV

        @pl.when(bounds_ref[0] < OWN_TILE - 2 * (distance - 1))
        def _(source=source, row=row, place=place):
            kv_buf[place : place + TOK_DEV, :] = source[row : row + TOK_DEV, :]
            for part in range(HALVES):
                piece = source[row + part * TILE : row + (part + 1) * TILE, :]
                kv_t[place // TILE + part] = piece.T

    def in_steps(low, step, carry):
        for size in STEPS:
            times = lax.div(OWN_TILE - low, size)
            carry = lax.fori_loop(
                0,
                times,
                lambda at, held, low=low, size=size: step(low + at * size, size, held),
                carry,
            )
            low = low + times * size
        return carry

    for half in range(HALVES):
        rows = slice(half * TILE, (half + 1) * TILE)
        lanes = slice(half * LANES, (half + 1) * LANES)
        lowest = bounds_ref[2 * half]
        first_full = bounds_ref[2 * half + 1]
        count = 1 + half
        own_part = slice(half * TILE, (half + count) * TILE)
        own_rows = slice(OWN_ROW, OWN_ROW + count * TILE)

        def score_masked(tile, row_max):
            kv_rows = tile_rows(tile, 1)
            raw = matmul(kv_buf[kv_rows, :HEAD_DIM], q_t[:, lanes])
            key_rel = tile * TILE + lax.broadcasted_iota(jnp.int32, raw.shape, 0)
            start_rel = jnp.concatenate([start_ref[:, rows]] * LOCAL, axis=1)
            raw = jnp.where(key_rel >= start_rel, raw, NEG)
            scores[kv_rows] = raw
            return jnp.maximum(row_max, jnp.max(by_sublane(raw), axis=0))

        def score_full(tile, count, row_max):
            kv_rows = tile_rows(tile, count)
            raw = matmul(kv_buf[kv_rows, :HEAD_DIM], q_t[:, lanes])
            scores[kv_rows] = raw
            return jnp.maximum(row_max, jnp.max(by_sublane(raw), axis=0))

        row_max = in_steps(first_full, score_full, max_ref[half * 8 : (half + 1) * 8])
        row_max = lax.fori_loop(lowest, first_full, score_masked, row_max)
        shift = jnp.max(row_max, axis=0, keepdims=True) * SCALE_LOG2

        def add_totals(carry, weights, prob_grad):
            total, dots = carry
            total = total + jnp.sum(by_sublane(weights), axis=0)
            dots = dots + jnp.sum(by_sublane(weights * prob_grad), axis=0)
            return total, dots

        def total_tile(tile, count, carry):
            kv_rows = tile_rows(tile, count)
            prob_grad = matmul(kv_buf[kv_rows, HEAD_DIM:], g_t[:, lanes])
            weights = jnp.exp2(scores[kv_rows] * SCALE_LOG2 - shift)
            scores[kv_rows] = weights
            grads[kv_rows] = prob_grad
            return add_totals(carry, weights, prob_grad)

        nothing = jnp.zeros((8, LANES), jnp.float32)
        weights = jnp.exp2(own_scores[own_part] * SCALE_LOG2 - shift)
        scores[own_rows] = weights
        carry = add_totals((nothing, nothing), weights, own_grads[own_part])
        total, dots = in_steps(lowest, total_tile, carry)
        inverse = 1.0 / jnp.sum(total, axis=0, keepdims=True)
        grad_dot = jnp.sum(dots, axis=0, keepdims=True) * inverse

        def score_grads(weights, prob_grad):
            weights = weights * inverse
            score_grad = (weights * (prob_grad - grad_dot)).astype(jnp.bfloat16)
            return weights.astype(jnp.bfloat16), score_grad

        def transposed_products(turned, prob, score_grad):
            out_add = dq_add = None
            for part, piece in enumerate(turned):
                inner = slice(part * TILE, (part + 1) * TILE)
                out_part = matmul(piece[HEAD_DIM:], prob[inner])
                dq_part = matmul(piece[:HEAD_DIM], score_grad[inner])
                out_add = out_part if part == 0 else out_add + out_part
                dq_add = dq_part if part == 0 else dq_add + dq_part
            return out_add, dq_add

        def backward_tile(tile, count, carry):
            kv_rows = tile_rows(tile, count)
            prob, score_grad = score_grads(scores[kv_rows], grads[kv_rows])
            kv_acc[kv_rows, HEAD_DIM:] += matmul(prob, g_cat[lanes])
            kv_acc[kv_rows, :HEAD_DIM] += matmul(score_grad, q_cat[lanes])
            turned = [kv_t[tile + part] for part in range(count)]
            out_add, dq_add = transposed_products(turned, prob, score_grad)
            o_acc[...] += out_add
            dq_acc[...] += dq_add
            return carry

        prob, score_grad = score_grads(scores[own_rows], own_grads[own_part])
        kv_acc[own_rows, HEAD_DIM:] += matmul(prob, g_cat[lanes])
        kv_acc[own_rows, :HEAD_DIM] += matmul(score_grad, q_cat[lanes])
        turned = [own_t[part] for part in range(count)]
        o_acc[...], dq_acc[...] = transposed_products(turned, prob, score_grad)
        in_steps(lowest, backward_tile, 0)
        for head in range(LOCAL):
            cols = slice(head * HEAD_DIM, (head + 1) * HEAD_DIM)
            place = slice(head * TILE, (head + 1) * TILE)
            out_ref[rows, cols] = o_acc[:, place].T.astype(jnp.bfloat16)
            dq_ref[rows, cols] = (dq_acc[:, place].T * SCALE).astype(jnp.bfloat16)

    def write_term(term, row, rows):
        keys = (kv_acc[row : row + rows, :HEAD_DIM] * SCALE).T.astype(term.dtype)
        values = kv_acc[row : row + rows, HEAD_DIM:].T.astype(term.dtype)
        for half in range(2):
            part = slice(half * HALF, (half + 1) * HALF)
            term[2 * half * HALF : (2 * half + 1) * HALF, :] = keys[part]
            term[(2 * half + 1) * HALF : (2 * half + 2) * HALF, :] = values[part]

    for distance, term in enumerate((t0, t1, t2, t3)):
        write_term(term, (WINDOW - distance) * TOK_DEV, TOK_DEV)
    write_term(t4a, 0, TILE)
    write_term(t4b, TILE, TILE)


def pick_kernel(
    place_ref, lengths_ref, keys_ref, values_ref,
    pair_ref, start_ref, bounds_ref, far_ref, lengths, sems,
):
    column = pl.multiple_of(place_ref[0], HEAD_DIM)
    copies = [pltpu.make_async_copy(lengths_ref, lengths, sems.at[2])]
    for place, source in enumerate((keys_ref, values_ref)):
        cols = pl.ds(place * HEAD_DIM, HEAD_DIM)
        copies.append(
            pltpu.make_async_copy(
                source.at[:, pl.ds(column, HEAD_DIM)], pair_ref.at[:, cols], sems.at[place]
            )
        )
    for copy in copies:
        copy.start()
    first_query = place_ref[1] * TOK_DEV
    origin = first_query - WINDOW * TOK_DEV
    lane_pos = first_query + lax.broadcasted_iota(jnp.int32, (1, TOK_DEV), 1)
    copies[0].wait()

    def next_doc(doc, carry):
        start, is_far, lane_start, edges = carry
        end = start + lengths[doc]
        reach = lax.div(end - 1, TOK_DEV) - lax.div(start, TOK_DEV)
        is_far = jnp.where((reach >= 3) & (doc != 1), 1, is_far)
        lane_start = jnp.where(lane_pos >= end, end, lane_start)
        edges = tuple(
            jnp.where(first_query + place >= end, end, edge)
            for place, edge in zip((0, TILE - 1, TILE, TOK_DEV - 1), edges)
        )
        return end, is_far, lane_start, edges

    zero = jnp.int32(0)
    _, is_far, lane_start, edges = lax.fori_loop(
        0, NDOCS, next_doc, (zero, zero, jnp.zeros((1, TOK_DEV), jnp.int32), (zero,) * 4), unroll=8
    )
    far_ref[0] = is_far
    start_ref[...] = lane_start - origin
    for half in range(HALVES):
        lowest = lax.div(edges[2 * half] - origin, TILE)
        full = lax.div(edges[2 * half + 1] - origin + TILE - 1, TILE)
        bounds_ref[2 * half] = jnp.minimum(lowest, OWN_TILE)
        bounds_ref[2 * half + 1] = jnp.minimum(full, OWN_TILE)
    for copy in copies[1:]:
        copy.wait()


def pick_block(place, lengths, keys, values):
    smem = pl.BlockSpec(memory_space=pltpu.SMEM)
    vmem = pl.BlockSpec(memory_space=pltpu.VMEM)
    anywhere = pl.BlockSpec(memory_space=pltpu.HBM)
    return pl.pallas_call(
        pick_kernel,
        out_shape=[
            jax.ShapeDtypeStruct((TOK_DEV, 2 * HEAD_DIM), jnp.bfloat16),
            jax.ShapeDtypeStruct((1, TOK_DEV), jnp.int32),
            jax.ShapeDtypeStruct((2 * HALVES,), jnp.int32),
            jax.ShapeDtypeStruct((1,), jnp.int32),
        ],
        in_specs=[smem, anywhere, anywhere, anywhere],
        out_specs=[vmem, vmem, smem, smem],
        scratch_shapes=[pltpu.SMEM((NDOCS,), jnp.int32), pltpu.SemaphoreType.DMA((3,))],
        compiler_params=pltpu.CompilerParams(vmem_limit_bytes=60 * 1024 * 1024),
        cost_estimate=pl.CostEstimate(flops=0, bytes_accessed=10**6, transcendentals=0),
        name="pick",
    )(place, lengths, keys, values)


def prepare(starts, queries, grads, pair):
    vmem = pl.BlockSpec(memory_space=pltpu.VMEM)
    own = jax.ShapeDtypeStruct((3 * TILE, LANES), jnp.float32)
    rows = jax.ShapeDtypeStruct((HALVES * LANES, HEAD_DIM), jnp.bfloat16)
    cols = jax.ShapeDtypeStruct((HEAD_DIM, HALVES * LANES), jnp.bfloat16)
    return pl.pallas_call(
        prepare_kernel,
        out_shape=[
            jax.ShapeDtypeStruct((8 * HALVES, LANES), jnp.float32),
            rows, rows, cols, cols, own, own,
            jax.ShapeDtypeStruct((HALVES, 2 * HEAD_DIM, TILE), jnp.bfloat16),
        ],
        in_specs=[vmem] * 4,
        out_specs=[vmem] * 8,
        compiler_params=pltpu.CompilerParams(vmem_limit_bytes=24 * 1024 * 1024),
        cost_estimate=pl.CostEstimate(
            flops=2 * 10**9, bytes_accessed=10**6, transcendentals=0
        ),
        name="prepare",
    )(starts, queries, grads, pair)


def attention_block(bounds, state, kv_blocks):
    vmem = pl.BlockSpec(memory_space=pltpu.VMEM)
    smem = pl.BlockSpec(memory_space=pltpu.SMEM)
    wide = jax.ShapeDtypeStruct((TOK_DEV, LOCAL * HEAD_DIM), jnp.bfloat16)
    own = jax.ShapeDtypeStruct((2 * HEAD_DIM, TOK_DEV), jnp.float32)
    term = jax.ShapeDtypeStruct((2 * HEAD_DIM, TOK_DEV), jnp.bfloat16)
    short = jax.ShapeDtypeStruct((2 * HEAD_DIM, TILE), jnp.bfloat16)
    return pl.pallas_call(
        attention_kernel,
        out_shape=[wide, wide, own, term, term, term, short, short],
        in_specs=[smem] + [vmem] * 13,
        out_specs=[vmem] * 8,
        scratch_shapes=[
            pltpu.VMEM((WINDOW * TOK_DEV, 2 * HEAD_DIM), jnp.bfloat16),
            pltpu.VMEM((OWN_TILE, 2 * HEAD_DIM, TILE), jnp.bfloat16),
            pltpu.VMEM((SPAN, LANES), jnp.float32),
            pltpu.VMEM((WINDOW * TOK_DEV, LANES), jnp.float32),
            pltpu.VMEM((SPAN, 2 * HEAD_DIM), jnp.float32),
            pltpu.VMEM((HEAD_DIM, LANES), jnp.float32),
            pltpu.VMEM((HEAD_DIM, LANES), jnp.float32),
        ],
        compiler_params=pltpu.CompilerParams(vmem_limit_bytes=40 * 1024 * 1024),
        cost_estimate=pl.CostEstimate(
            flops=5 * 10**9, bytes_accessed=4 * 10**6, transcendentals=6 * 10**6
        ),
        name="attention",
    )(bounds, *state, *kv_blocks)


def moved(value, pairs):
    return lax.ppermute(value, "ctx", pairs)


def from_partner(value, axis, apart):
    mask = 2**apart
    pairs = [(source, source ^ mask) for source in range(lax.axis_size(axis))]
    return lax.ppermute(value, axis, pairs)


def pairs_at(distance, count):
    return [(source, source + distance) for source in range(count - distance)]


def needed(source, target):
    return target < 5 or source >= 4


def reversed_pairs(pairs):
    return [(target, source) for source, target in pairs]


def shards(query_states, key_states, value_states, out_grad, lengths):
    count = lax.axis_size("ctx")
    block_index = lax.axis_index("ctx")
    head_index = lax.axis_index("head")
    kv_start = head_index * LOCAL // (HEADS // KV_HEADS) * HEAD_DIM
    own_half = head_index % 2
    place = jnp.stack([kv_start.astype(jnp.int32), block_index.astype(jnp.int32)])
    own_pair, starts, bounds, far_flag = pick_block(place, lengths, key_states, value_states)
    near = {
        distance: [pair for pair in pairs_at(distance, count) if needed(*pair)]
        for distance in (1, 2)
    }
    near[3] = [(0, 3), (1, 4)]
    near[4] = [(0, 4)]
    wide = {distance: pairs_at(distance, count)[WINDOW:] for distance in (3, 4)}
    is_far = far_flag[0] == 1
    far_fourth = lax.cond(is_far, lambda pair: moved(pair, wide[4]), lambda pair: pair, own_pair)
    second = moved(own_pair, pairs_at(2, count))
    fourth = moved(own_pair, [(0, 4), (1, 5)])
    own_pair, far_fourth = lax.optimization_barrier((own_pair, far_fourth))
    state = prepare(starts, query_states, out_grad, own_pair)
    second, fourth, highest = lax.optimization_barrier((second, fourth, state[0]))
    state = [starts, highest] + list(state[1:])
    fourth = jnp.where(block_index < 6, fourth, far_fourth)
    is_even = block_index % 2 == 0
    outbound = jnp.concatenate(
        [jnp.where(is_even, own_pair, second), jnp.where(is_even, second, fourth)], axis=0
    )
    swapped = moved(outbound, [(place, place ^ 1) for place in range(count)])
    attended, query_grad, t0, t1, t2, t3, t4a, t4b = attention_block(
        bounds, state, [own_pair, second, swapped, fourth]
    )
    back4 = moved(t4b, reversed_pairs(near[4]))
    back3 = moved(t3, reversed_pairs(near[3]))
    back2 = moved(t2, reversed_pairs(near[2]))
    back1 = moved(t1, reversed_pairs(near[1]))
    gathered = t0 + back3.astype(jnp.float32)
    gathered = gathered + jnp.pad(back4, ((0, 0), (TILE, 0))).astype(jnp.float32)
    gathered = lax.optimization_barrier(gathered)
    gathered = gathered + back2.astype(jnp.float32) + back1.astype(jnp.float32)

    def with_far(total, third_term, low_term, high_term):
        fourth_term = jnp.concatenate([low_term, high_term], axis=1)
        from3 = moved(third_term, reversed_pairs(wide[3]))
        from4 = moved(fourth_term, reversed_pairs(wide[4]))
        return total + from3.astype(jnp.float32) + from4.astype(jnp.float32)

    gathered = lax.cond(
        is_far, with_far, lambda total, *others: total, gathered, t3, t4a, t4b
    )
    outgoing = lax.dynamic_slice_in_dim(gathered, (1 - own_half) * HEAD_DIM, HEAD_DIM, 0)
    received = from_partner(outgoing.astype(jnp.bfloat16), "head", 0).astype(jnp.float32)
    kept = lax.dynamic_slice_in_dim(gathered, own_half * HEAD_DIM, HEAD_DIM, 0)
    both = (kept + received).astype(jnp.bfloat16)
    return attended, query_grad, both[:HALF].T, both[HALF:].T


def solution(mesh):
    return jax.shard_map(
        shards,
        mesh=mesh,
        in_specs=(P("ctx", "head"), P("ctx", None), P("ctx", None), P("ctx", "head"), P()),
        out_specs=(P("ctx", "head"), P("ctx", "head"), P("ctx", "head"), P("ctx", "head")),
        check_vma=False,
    )
```

```python
import math

import jax
import jax.numpy as jnp
from jax import lax
from jax.experimental import pallas as pl
from jax.experimental.pallas import tpu as pltpu
from jax.sharding import PartitionSpec as P

HEAD_DIM = 128
HEADS = 16
KV_HEADS = 2
WINDOW = 4
TOK_DEV = 512
NDOCS = 64
LOCAL = 4
HALF = HEAD_DIM // 2
TILE = 256
SPAN = (WINDOW + 1) * TOK_DEV
HALVES = TOK_DEV // TILE
OWN_ROW = WINDOW * TOK_DEV
OWN_TILE = OWN_ROW // TILE
LANES = LOCAL * TILE
SCALE = HEAD_DIM ** (-0.5)
SCALE_LOG2 = SCALE * math.log2(math.e)
NEG = -1e30
STEPS = (5, 2, 1)


def contract_last(first_matrix, second_matrix):
    return lax.dot_general(
        first_matrix, second_matrix, (((1,), (1,)), ((), ())), preferred_element_type=jnp.float32
    )


def matmul(first_matrix, second_matrix):
    return jnp.dot(first_matrix, second_matrix, preferred_element_type=jnp.float32)


def tile_rows(tile, count):
    return pl.ds(pl.multiple_of(tile * TILE, TILE), count * TILE)


def by_sublane(array):
    return array.reshape(array.shape[0] // 8, 8, LANES)


def prepare_kernel(
    start_ref, q_ref, grad_ref, pair_ref,
    max_ref, q_cat, g_cat, q_t, g_t, own_scores, own_grads, own_t,
):
    for part in range(HALVES):
        own_t[part] = pair_ref[part * TILE : (part + 1) * TILE, :].T
    for half in range(HALVES):
        rows = slice(half * TILE, (half + 1) * TILE)
        lanes = slice(half * LANES, (half + 1) * LANES)
        for head in range(LOCAL):
            cols = slice(head * HEAD_DIM, (head + 1) * HEAD_DIM)
            place = slice(half * LANES + head * TILE, half * LANES + (head + 1) * TILE)
            q_cat[place, :] = q_ref[rows, cols]
            g_cat[place, :] = grad_ref[rows, cols]
            q_t[:, place] = q_ref[rows, cols].T
            g_t[:, place] = grad_ref[rows, cols].T
        start_rel = jnp.concatenate([start_ref[:, rows] - OWN_ROW] * LOCAL, axis=1)
        lane = lax.broadcasted_iota(jnp.int32, (1, TILE), 1)
        query_rel = jnp.concatenate([lane + half * TILE] * LOCAL, axis=1)
        count = 1 + half
        own_rows = slice(half * TILE, (half + count) * TILE)
        keys = pair_ref[: count * TILE, :HEAD_DIM]
        values = pair_ref[: count * TILE, HEAD_DIM:]
        raw = matmul(keys, q_t[:, lanes])
        key_rel = lax.broadcasted_iota(jnp.int32, raw.shape, 0)
        raw = jnp.where((key_rel >= start_rel) & (key_rel <= query_rel), raw, NEG)
        own_scores[own_rows] = raw
        max_ref[half * 8 : (half + 1) * 8] = jnp.max(by_sublane(raw), axis=0)
        own_grads[own_rows] = matmul(values, g_t[:, lanes])


def attention_kernel(
    bounds_ref, start_ref, max_ref, q_cat, g_cat, q_t, g_t, own_scores, own_grads, own_t,
    pair_ref, kv2_ref, kv13_ref, kv4_ref,
    out_ref, dq_ref, t0, t1, t2, t3, t4a, t4b,
    kv_buf, kv_t, scores, grads, kv_acc, o_acc, dq_acc,
):
    kv_acc[...] = jnp.zeros_like(kv_acc)
    sources = (
        (1, kv13_ref, 0), (2, kv2_ref, 0), (3, kv13_ref, TOK_DEV), (4, kv4_ref, 0)
    )
    for distance, source, row in sources:
        place = (WINDOW - distance) * TOK_DEV

        @pl.when(bounds_ref[0] < OWN_TILE - 2 * (distance - 1))
        def _(source=source, row=row, place=place):
            kv_buf[place : place + TOK_DEV, :] = source[row : row + TOK_DEV, :]
            for part in range(HALVES):
                piece = source[row + part * TILE : row + (part + 1) * TILE, :]
                kv_t[place // TILE + part] = piece.T

    def in_steps(low, step, carry):
        for size in STEPS:
            times = lax.div(OWN_TILE - low, size)
            carry = lax.fori_loop(
                0,
                times,
                lambda at, held, low=low, size=size: step(low + at * size, size, held),
                carry,
            )
            low = low + times * size
        return carry

    for half in range(HALVES):
        rows = slice(half * TILE, (half + 1) * TILE)
        lanes = slice(half * LANES, (half + 1) * LANES)
        lowest = bounds_ref[2 * half]
        first_full = bounds_ref[2 * half + 1]
        count = 1 + half
        own_part = slice(half * TILE, (half + count) * TILE)
        own_rows = slice(OWN_ROW, OWN_ROW + count * TILE)

        def score_masked(tile, row_max):
            kv_rows = tile_rows(tile, 1)
            raw = matmul(kv_buf[kv_rows, :HEAD_DIM], q_t[:, lanes])
            key_rel = tile * TILE + lax.broadcasted_iota(jnp.int32, raw.shape, 0)
            start_rel = jnp.concatenate([start_ref[:, rows]] * LOCAL, axis=1)
            raw = jnp.where(key_rel >= start_rel, raw, NEG)
            scores[kv_rows] = raw
            return jnp.maximum(row_max, jnp.max(by_sublane(raw), axis=0))

        def score_full(tile, count, row_max):
            kv_rows = tile_rows(tile, count)
            raw = matmul(kv_buf[kv_rows, :HEAD_DIM], q_t[:, lanes])
            scores[kv_rows] = raw
            return jnp.maximum(row_max, jnp.max(by_sublane(raw), axis=0))

        row_max = in_steps(first_full, score_full, max_ref[half * 8 : (half + 1) * 8])
        row_max = lax.fori_loop(lowest, first_full, score_masked, row_max)
        shift = jnp.max(row_max, axis=0, keepdims=True) * SCALE_LOG2

        def add_totals(carry, weights, prob_grad):
            total, dots = carry
            total = total + jnp.sum(by_sublane(weights), axis=0)
            dots = dots + jnp.sum(by_sublane(weights * prob_grad), axis=0)
            return total, dots

        def total_tile(tile, count, carry):
            kv_rows = tile_rows(tile, count)
            prob_grad = matmul(kv_buf[kv_rows, HEAD_DIM:], g_t[:, lanes])
            weights = jnp.exp2(scores[kv_rows] * SCALE_LOG2 - shift)
            scores[kv_rows] = weights
            grads[kv_rows] = prob_grad
            return add_totals(carry, weights, prob_grad)

        nothing = jnp.zeros((8, LANES), jnp.float32)
        weights = jnp.exp2(own_scores[own_part] * SCALE_LOG2 - shift)
        scores[own_rows] = weights
        carry = add_totals((nothing, nothing), weights, own_grads[own_part])
        total, dots = in_steps(lowest, total_tile, carry)
        inverse = 1.0 / jnp.sum(total, axis=0, keepdims=True)
        grad_dot = jnp.sum(dots, axis=0, keepdims=True) * inverse

        def score_grads(weights, prob_grad):
            weights = weights * inverse
            score_grad = (weights * (prob_grad - grad_dot)).astype(jnp.bfloat16)
            return weights.astype(jnp.bfloat16), score_grad

        def transposed_products(turned, prob, score_grad):
            out_add = dq_add = None
            for part, piece in enumerate(turned):
                inner = slice(part * TILE, (part + 1) * TILE)
                out_part = matmul(piece[HEAD_DIM:], prob[inner])
                dq_part = matmul(piece[:HEAD_DIM], score_grad[inner])
                out_add = out_part if part == 0 else out_add + out_part
                dq_add = dq_part if part == 0 else dq_add + dq_part
            return out_add, dq_add

        def backward_tile(tile, count, carry):
            kv_rows = tile_rows(tile, count)
            prob, score_grad = score_grads(scores[kv_rows], grads[kv_rows])
            kv_acc[kv_rows, HEAD_DIM:] += matmul(prob, g_cat[lanes])
            kv_acc[kv_rows, :HEAD_DIM] += matmul(score_grad, q_cat[lanes])
            turned = [kv_t[tile + part] for part in range(count)]
            out_add, dq_add = transposed_products(turned, prob, score_grad)
            o_acc[...] += out_add
            dq_acc[...] += dq_add
            return carry

        prob, score_grad = score_grads(scores[own_rows], own_grads[own_part])
        kv_acc[own_rows, HEAD_DIM:] += matmul(prob, g_cat[lanes])
        kv_acc[own_rows, :HEAD_DIM] += matmul(score_grad, q_cat[lanes])
        turned = [own_t[part] for part in range(count)]
        o_acc[...], dq_acc[...] = transposed_products(turned, prob, score_grad)
        in_steps(lowest, backward_tile, 0)
        for head in range(LOCAL):
            cols = slice(head * HEAD_DIM, (head + 1) * HEAD_DIM)
            place = slice(head * TILE, (head + 1) * TILE)
            out_ref[rows, cols] = o_acc[:, place].T.astype(jnp.bfloat16)
            dq_ref[rows, cols] = (dq_acc[:, place].T * SCALE).astype(jnp.bfloat16)

    def write_term(term, row, rows):
        keys = (kv_acc[row : row + rows, :HEAD_DIM] * SCALE).T.astype(term.dtype)
        values = kv_acc[row : row + rows, HEAD_DIM:].T.astype(term.dtype)
        for half in range(2):
            part = slice(half * HALF, (half + 1) * HALF)
            term[2 * half * HALF : (2 * half + 1) * HALF, :] = keys[part]
            term[(2 * half + 1) * HALF : (2 * half + 2) * HALF, :] = values[part]

    for distance, term in enumerate((t0, t1, t2, t3)):
        write_term(term, (WINDOW - distance) * TOK_DEV, TOK_DEV)
    write_term(t4a, 0, TILE)
    write_term(t4b, TILE, TILE)


def pick_kernel(column_ref, keys_ref, values_ref, pair_ref, sems):
    column = pl.multiple_of(column_ref[0], HEAD_DIM)
    copies = []
    for place, source in enumerate((keys_ref, values_ref)):
        cols = pl.ds(place * HEAD_DIM, HEAD_DIM)
        copies.append(
            pltpu.make_async_copy(
                source.at[:, pl.ds(column, HEAD_DIM)], pair_ref.at[:, cols], sems.at[place]
            )
        )
    for copy in copies:
        copy.start()
    for copy in copies:
        copy.wait()


def pick_block(column, keys, values):
    smem = pl.BlockSpec(memory_space=pltpu.SMEM)
    vmem = pl.BlockSpec(memory_space=pltpu.VMEM)
    anywhere = pl.BlockSpec(memory_space=pltpu.HBM)
    return pl.pallas_call(
        pick_kernel,
        out_shape=jax.ShapeDtypeStruct((TOK_DEV, 2 * HEAD_DIM), jnp.bfloat16),
        in_specs=[smem, anywhere, anywhere],
        out_specs=vmem,
        scratch_shapes=[pltpu.SemaphoreType.DMA((2,))],
        compiler_params=pltpu.CompilerParams(vmem_limit_bytes=60 * 1024 * 1024),
        cost_estimate=pl.CostEstimate(flops=0, bytes_accessed=10**6, transcendentals=0),
        name="pick",
    )(column, keys, values)


def scan_kernel(lengths_ref, block_ref, start_ref, bounds_ref, far_ref):
    first_query = block_ref[0] * TOK_DEV
    origin = first_query - WINDOW * TOK_DEV
    lane_pos = first_query + lax.broadcasted_iota(jnp.int32, (1, TOK_DEV), 1)

    def next_doc(doc, carry):
        start, is_far, lane_start, edges = carry
        end = start + lengths_ref[doc]
        reach = lax.div(end - 1, TOK_DEV) - lax.div(start, TOK_DEV)
        is_far = jnp.where((reach >= 3) & (doc != 1), 1, is_far)
        lane_start = jnp.where(lane_pos >= end, end, lane_start)
        edges = tuple(
            jnp.where(first_query + place >= end, end, edge)
            for place, edge in zip((0, TILE - 1, TILE, TOK_DEV - 1), edges)
        )
        return end, is_far, lane_start, edges

    zero = jnp.int32(0)
    _, is_far, lane_start, edges = lax.fori_loop(
        0, NDOCS, next_doc, (zero, zero, jnp.zeros((1, TOK_DEV), jnp.int32), (zero,) * 4), unroll=8
    )
    far_ref[0] = is_far
    start_ref[...] = lane_start - origin
    for half in range(HALVES):
        lowest = lax.div(edges[2 * half] - origin, TILE)
        full = lax.div(edges[2 * half + 1] - origin + TILE - 1, TILE)
        bounds_ref[2 * half] = jnp.minimum(lowest, OWN_TILE)
        bounds_ref[2 * half + 1] = jnp.minimum(full, OWN_TILE)


def scan_documents(lengths, block):
    smem = pl.BlockSpec(memory_space=pltpu.SMEM)
    vmem = pl.BlockSpec(memory_space=pltpu.VMEM)
    return pl.pallas_call(
        scan_kernel,
        out_shape=[
            jax.ShapeDtypeStruct((1, TOK_DEV), jnp.int32),
            jax.ShapeDtypeStruct((2 * HALVES,), jnp.int32),
            jax.ShapeDtypeStruct((1,), jnp.int32),
        ],
        in_specs=[smem, smem],
        out_specs=[vmem, smem, smem],
        cost_estimate=pl.CostEstimate(flops=10**6, bytes_accessed=10**4, transcendentals=0),
        name="scan",
    )(lengths, block)


def prepare(starts, queries, grads, pair):
    vmem = pl.BlockSpec(memory_space=pltpu.VMEM)
    own = jax.ShapeDtypeStruct((3 * TILE, LANES), jnp.float32)
    rows = jax.ShapeDtypeStruct((HALVES * LANES, HEAD_DIM), jnp.bfloat16)
    cols = jax.ShapeDtypeStruct((HEAD_DIM, HALVES * LANES), jnp.bfloat16)
    return pl.pallas_call(
        prepare_kernel,
        out_shape=[
            jax.ShapeDtypeStruct((8 * HALVES, LANES), jnp.float32),
            rows, rows, cols, cols, own, own,
            jax.ShapeDtypeStruct((HALVES, 2 * HEAD_DIM, TILE), jnp.bfloat16),
        ],
        in_specs=[vmem] * 4,
        out_specs=[vmem] * 8,
        compiler_params=pltpu.CompilerParams(vmem_limit_bytes=24 * 1024 * 1024),
        cost_estimate=pl.CostEstimate(
            flops=2 * 10**9, bytes_accessed=10**6, transcendentals=0
        ),
        name="prepare",
    )(starts, queries, grads, pair)


def attention_block(bounds, state, kv_blocks):
    vmem = pl.BlockSpec(memory_space=pltpu.VMEM)
    smem = pl.BlockSpec(memory_space=pltpu.SMEM)
    wide = jax.ShapeDtypeStruct((TOK_DEV, LOCAL * HEAD_DIM), jnp.bfloat16)
    own = jax.ShapeDtypeStruct((2 * HEAD_DIM, TOK_DEV), jnp.float32)
    term = jax.ShapeDtypeStruct((2 * HEAD_DIM, TOK_DEV), jnp.bfloat16)
    short = jax.ShapeDtypeStruct((2 * HEAD_DIM, TILE), jnp.bfloat16)
    return pl.pallas_call(
        attention_kernel,
        out_shape=[wide, wide, own, term, term, term, short, short],
        in_specs=[smem] + [vmem] * 13,
        out_specs=[vmem] * 8,
        scratch_shapes=[
            pltpu.VMEM((WINDOW * TOK_DEV, 2 * HEAD_DIM), jnp.bfloat16),
            pltpu.VMEM((OWN_TILE, 2 * HEAD_DIM, TILE), jnp.bfloat16),
            pltpu.VMEM((SPAN, LANES), jnp.float32),
            pltpu.VMEM((WINDOW * TOK_DEV, LANES), jnp.float32),
            pltpu.VMEM((SPAN, 2 * HEAD_DIM), jnp.float32),
            pltpu.VMEM((HEAD_DIM, LANES), jnp.float32),
            pltpu.VMEM((HEAD_DIM, LANES), jnp.float32),
        ],
        compiler_params=pltpu.CompilerParams(vmem_limit_bytes=40 * 1024 * 1024),
        cost_estimate=pl.CostEstimate(
            flops=5 * 10**9, bytes_accessed=4 * 10**6, transcendentals=6 * 10**6
        ),
        name="attention",
    )(bounds, *state, *kv_blocks)


def moved(value, pairs):
    return lax.ppermute(value, "ctx", pairs)


def from_partner(value, axis, apart):
    mask = 2**apart
    pairs = [(source, source ^ mask) for source in range(lax.axis_size(axis))]
    return lax.ppermute(value, axis, pairs)


def pairs_at(distance, count):
    return [(source, source + distance) for source in range(count - distance)]


def needed(source, target):
    return target < 5 or source >= 4


def reversed_pairs(pairs):
    return [(target, source) for source, target in pairs]


def shards(query_states, key_states, value_states, out_grad, lengths):
    count = lax.axis_size("ctx")
    block_index = lax.axis_index("ctx")
    head_index = lax.axis_index("head")
    kv_start = head_index * LOCAL // (HEADS // KV_HEADS) * HEAD_DIM
    own_half = head_index % 2
    own_pair = pick_block(kv_start.astype(jnp.int32).reshape(1), key_states, value_states)
    starts, bounds, far_flag = scan_documents(lengths, block_index.astype(jnp.int32).reshape(1))
    near = {
        distance: [pair for pair in pairs_at(distance, count) if needed(*pair)]
        for distance in (1, 2)
    }
    near[3] = [(0, 3), (1, 4)]
    near[4] = [(0, 4)]
    wide = {distance: pairs_at(distance, count)[WINDOW:] for distance in (3, 4)}
    is_far = far_flag[0] == 1
    far_fourth = lax.cond(is_far, lambda pair: moved(pair, wide[4]), lambda pair: pair, own_pair)
    second = moved(own_pair, pairs_at(2, count))
    fourth = moved(own_pair, [(0, 4), (1, 5)])
    own_pair, far_fourth = lax.optimization_barrier((own_pair, far_fourth))
    state = prepare(starts, query_states, out_grad, own_pair)
    second, fourth, highest = lax.optimization_barrier((second, fourth, state[0]))
    state = [starts, highest] + list(state[1:])
    fourth = jnp.where(block_index < 6, fourth, far_fourth)
    is_even = block_index % 2 == 0
    outbound = jnp.concatenate(
        [jnp.where(is_even, own_pair, second), jnp.where(is_even, second, fourth)], axis=0
    )
    swapped = moved(outbound, [(place, place ^ 1) for place in range(count)])
    attended, query_grad, t0, t1, t2, t3, t4a, t4b = attention_block(
        bounds, state, [own_pair, second, swapped, fourth]
    )
    back4 = moved(t4b, reversed_pairs(near[4]))
    back3 = moved(t3, reversed_pairs(near[3]))
    back2 = moved(t2, reversed_pairs(near[2]))
    back1 = moved(t1, reversed_pairs(near[1]))
    gathered = t0 + back3.astype(jnp.float32)
    gathered = gathered + jnp.pad(back4, ((0, 0), (TILE, 0))).astype(jnp.float32)
    gathered = lax.optimization_barrier(gathered)
    gathered = gathered + back2.astype(jnp.float32) + back1.astype(jnp.float32)

    def with_far(total, third_term, low_term, high_term):
        fourth_term = jnp.concatenate([low_term, high_term], axis=1)
        from3 = moved(third_term, reversed_pairs(wide[3]))
        from4 = moved(fourth_term, reversed_pairs(wide[4]))
        return total + from3.astype(jnp.float32) + from4.astype(jnp.float32)

    gathered = lax.cond(
        is_far, with_far, lambda total, *others: total, gathered, t3, t4a, t4b
    )
    outgoing = lax.dynamic_slice_in_dim(gathered, (1 - own_half) * HEAD_DIM, HEAD_DIM, 0)
    received = from_partner(outgoing.astype(jnp.bfloat16), "head", 0).astype(jnp.float32)
    kept = lax.dynamic_slice_in_dim(gathered, own_half * HEAD_DIM, HEAD_DIM, 0)
    both = (kept + received).astype(jnp.bfloat16)
    return attended, query_grad, both[:HALF].T, both[HALF:].T


def solution(mesh):
    return jax.shard_map(
        shards,
        mesh=mesh,
        in_specs=(P("ctx", "head"), P("ctx", None), P("ctx", None), P("ctx", "head"), P()),
        out_specs=(P("ctx", "head"), P("ctx", "head"), P("ctx", "head"), P("ctx", "head")),
        check_vma=False,
    )
```

```python
import math

import jax
import jax.numpy as jnp
from jax import lax
from jax.experimental import pallas as pl
from jax.experimental.pallas import tpu as pltpu
from jax.sharding import PartitionSpec as P

HEAD_DIM = 128
HEADS = 16
KV_HEADS = 2
WINDOW = 4
TOK_DEV = 512
NDOCS = 64
LOCAL = 4
HALF = HEAD_DIM // 2
TILE = 256
SPAN = (WINDOW + 1) * TOK_DEV
HALVES = TOK_DEV // TILE
OWN_ROW = WINDOW * TOK_DEV
OWN_TILE = OWN_ROW // TILE
LANES = LOCAL * TILE
SCALE = HEAD_DIM ** (-0.5)
SCALE_LOG2 = SCALE * math.log2(math.e)
NEG = -1e30
STEPS = (5, 2, 1)


def contract_last(first_matrix, second_matrix):
    return lax.dot_general(
        first_matrix, second_matrix, (((1,), (1,)), ((), ())), preferred_element_type=jnp.float32
    )


def matmul(first_matrix, second_matrix):
    return jnp.dot(first_matrix, second_matrix, preferred_element_type=jnp.float32)


def tile_rows(tile, count):
    return pl.ds(pl.multiple_of(tile * TILE, TILE), count * TILE)


def by_sublane(array):
    return array.reshape(array.shape[0] // 8, 8, LANES)


def prepare_kernel(
    start_ref, q_ref, grad_ref, pair_ref,
    max_ref, q_cat, g_cat, q_t, g_t, own_scores, own_grads, own_t,
):
    for part in range(HALVES):
        own_t[part] = pair_ref[part * TILE : (part + 1) * TILE, :].T
    for half in range(HALVES):
        rows = slice(half * TILE, (half + 1) * TILE)
        lanes = slice(half * LANES, (half + 1) * LANES)
        for head in range(LOCAL):
            cols = slice(head * HEAD_DIM, (head + 1) * HEAD_DIM)
            place = slice(half * LANES + head * TILE, half * LANES + (head + 1) * TILE)
            q_cat[place, :] = q_ref[rows, cols]
            g_cat[place, :] = grad_ref[rows, cols]
            q_t[:, place] = q_ref[rows, cols].T
            g_t[:, place] = grad_ref[rows, cols].T
        start_rel = jnp.concatenate([start_ref[:, rows] - OWN_ROW] * LOCAL, axis=1)
        lane = lax.broadcasted_iota(jnp.int32, (1, TILE), 1)
        query_rel = jnp.concatenate([lane + half * TILE] * LOCAL, axis=1)
        count = 1 + half
        own_rows = slice(half * TILE, (half + count) * TILE)
        keys = pair_ref[: count * TILE, :HEAD_DIM]
        values = pair_ref[: count * TILE, HEAD_DIM:]
        raw = matmul(keys, q_t[:, lanes])
        key_rel = lax.broadcasted_iota(jnp.int32, raw.shape, 0)
        raw = jnp.where((key_rel >= start_rel) & (key_rel <= query_rel), raw, NEG)
        own_scores[own_rows] = raw
        max_ref[half * 8 : (half + 1) * 8] = jnp.max(by_sublane(raw), axis=0)
        own_grads[own_rows] = matmul(values, g_t[:, lanes])


def attention_kernel(
    bounds_ref, start_ref, max_ref, q_cat, g_cat, q_t, g_t, own_scores, own_grads, own_t,
    pair_ref, kv2_ref, kv13_ref, kv4_ref,
    out_ref, dq_ref, t0, t1, t2, t3, t4a, t4b,
    kv_buf, kv_t, scores, grads, kv_acc, o_acc, dq_acc,
):
    kv_acc[...] = jnp.zeros_like(kv_acc)
    sources = (
        (1, kv13_ref, 0), (2, kv2_ref, 0), (3, kv13_ref, TOK_DEV), (4, kv4_ref, 0)
    )
    for distance, source, row in sources:
        place = (WINDOW - distance) * TOK_DEV

        @pl.when(bounds_ref[0] < OWN_TILE - 2 * (distance - 1))
        def _(source=source, row=row, place=place):
            kv_buf[place : place + TOK_DEV, :] = source[row : row + TOK_DEV, :]
            for part in range(HALVES):
                piece = source[row + part * TILE : row + (part + 1) * TILE, :]
                kv_t[place // TILE + part] = piece.T

    def in_steps(low, step, carry):
        for size in STEPS:
            times = lax.div(OWN_TILE - low, size)
            carry = lax.fori_loop(
                0,
                times,
                lambda at, held, low=low, size=size: step(low + at * size, size, held),
                carry,
            )
            low = low + times * size
        return carry

    for half in range(HALVES):
        rows = slice(half * TILE, (half + 1) * TILE)
        lanes = slice(half * LANES, (half + 1) * LANES)
        lowest = bounds_ref[2 * half]
        first_full = bounds_ref[2 * half + 1]
        count = 1 + half
        own_part = slice(half * TILE, (half + count) * TILE)
        own_rows = slice(OWN_ROW, OWN_ROW + count * TILE)

        def score_masked(tile, row_max):
            kv_rows = tile_rows(tile, 1)
            raw = matmul(kv_buf[kv_rows, :HEAD_DIM], q_t[:, lanes])
            key_rel = tile * TILE + lax.broadcasted_iota(jnp.int32, raw.shape, 0)
            start_rel = jnp.concatenate([start_ref[:, rows]] * LOCAL, axis=1)
            raw = jnp.where(key_rel >= start_rel, raw, NEG)
            scores[kv_rows] = raw
            return jnp.maximum(row_max, jnp.max(by_sublane(raw), axis=0))

        def score_full(tile, count, row_max):
            kv_rows = tile_rows(tile, count)
            raw = matmul(kv_buf[kv_rows, :HEAD_DIM], q_t[:, lanes])
            scores[kv_rows] = raw
            return jnp.maximum(row_max, jnp.max(by_sublane(raw), axis=0))

        row_max = in_steps(first_full, score_full, max_ref[half * 8 : (half + 1) * 8])
        row_max = lax.fori_loop(lowest, first_full, score_masked, row_max)
        shift = jnp.max(row_max, axis=0, keepdims=True) * SCALE_LOG2

        def add_totals(carry, weights, prob_grad):
            total, dots = carry
            total = total + jnp.sum(by_sublane(weights), axis=0)
            dots = dots + jnp.sum(by_sublane(weights * prob_grad), axis=0)
            return total, dots

        def total_tile(tile, count, carry):
            kv_rows = tile_rows(tile, count)
            prob_grad = matmul(kv_buf[kv_rows, HEAD_DIM:], g_t[:, lanes])
            weights = jnp.exp2(scores[kv_rows] * SCALE_LOG2 - shift)
            scores[kv_rows] = weights
            grads[kv_rows] = prob_grad
            return add_totals(carry, weights, prob_grad)

        nothing = jnp.zeros((8, LANES), jnp.float32)
        weights = jnp.exp2(own_scores[own_part] * SCALE_LOG2 - shift)
        scores[own_rows] = weights
        carry = add_totals((nothing, nothing), weights, own_grads[own_part])
        total, dots = in_steps(lowest, total_tile, carry)
        inverse = 1.0 / jnp.sum(total, axis=0, keepdims=True)
        grad_dot = jnp.sum(dots, axis=0, keepdims=True) * inverse

        def score_grads(weights, prob_grad):
            weights = weights * inverse
            score_grad = (weights * (prob_grad - grad_dot)).astype(jnp.bfloat16)
            return weights.astype(jnp.bfloat16), score_grad

        def transposed_products(turned, prob, score_grad):
            out_add = dq_add = None
            for part, piece in enumerate(turned):
                inner = slice(part * TILE, (part + 1) * TILE)
                out_part = matmul(piece[HEAD_DIM:], prob[inner])
                dq_part = matmul(piece[:HEAD_DIM], score_grad[inner])
                out_add = out_part if part == 0 else out_add + out_part
                dq_add = dq_part if part == 0 else dq_add + dq_part
            return out_add, dq_add

        def backward_tile(tile, count, carry):
            kv_rows = tile_rows(tile, count)
            prob, score_grad = score_grads(scores[kv_rows], grads[kv_rows])
            kv_acc[kv_rows, HEAD_DIM:] += matmul(prob, g_cat[lanes])
            kv_acc[kv_rows, :HEAD_DIM] += matmul(score_grad, q_cat[lanes])
            turned = [kv_t[tile + part] for part in range(count)]
            out_add, dq_add = transposed_products(turned, prob, score_grad)
            o_acc[...] += out_add
            dq_acc[...] += dq_add
            return carry

        prob, score_grad = score_grads(scores[own_rows], own_grads[own_part])
        kv_acc[own_rows, HEAD_DIM:] += matmul(prob, g_cat[lanes])
        kv_acc[own_rows, :HEAD_DIM] += matmul(score_grad, q_cat[lanes])
        turned = [own_t[part] for part in range(count)]
        o_acc[...], dq_acc[...] = transposed_products(turned, prob, score_grad)
        in_steps(lowest, backward_tile, 0)
        for head in range(LOCAL):
            cols = slice(head * HEAD_DIM, (head + 1) * HEAD_DIM)
            place = slice(head * TILE, (head + 1) * TILE)
            out_ref[rows, cols] = o_acc[:, place].T.astype(jnp.bfloat16)
            dq_ref[rows, cols] = (dq_acc[:, place].T * SCALE).astype(jnp.bfloat16)

    def write_term(term, row, rows):
        keys = (kv_acc[row : row + rows, :HEAD_DIM] * SCALE).T.astype(term.dtype)
        values = kv_acc[row : row + rows, HEAD_DIM:].T.astype(term.dtype)
        for half in range(2):
            part = slice(half * HALF, (half + 1) * HALF)
            term[2 * half * HALF : (2 * half + 1) * HALF, :] = keys[part]
            term[(2 * half + 1) * HALF : (2 * half + 2) * HALF, :] = values[part]

    for distance, term in enumerate((t0, t1, t2, t3)):
        write_term(term, (WINDOW - distance) * TOK_DEV, TOK_DEV)
    write_term(t4a, 0, TILE)
    write_term(t4b, TILE, TILE)


def pick_kernel(column_ref, keys_ref, values_ref, pair_ref, sems):
    column = pl.multiple_of(column_ref[0], HEAD_DIM)
    copies = []
    for place, source in enumerate((keys_ref, values_ref)):
        cols = pl.ds(place * HEAD_DIM, HEAD_DIM)
        copies.append(
            pltpu.make_async_copy(
                source.at[:, pl.ds(column, HEAD_DIM)], pair_ref.at[:, cols], sems.at[place]
            )
        )
    for copy in copies:
        copy.start()
    for copy in copies:
        copy.wait()


def pick_block(column, keys, values):
    smem = pl.BlockSpec(memory_space=pltpu.SMEM)
    vmem = pl.BlockSpec(memory_space=pltpu.VMEM)
    anywhere = pl.BlockSpec(memory_space=pltpu.HBM)
    return pl.pallas_call(
        pick_kernel,
        out_shape=jax.ShapeDtypeStruct((TOK_DEV, 2 * HEAD_DIM), jnp.bfloat16),
        in_specs=[smem, anywhere, anywhere],
        out_specs=vmem,
        scratch_shapes=[pltpu.SemaphoreType.DMA((2,))],
        compiler_params=pltpu.CompilerParams(vmem_limit_bytes=60 * 1024 * 1024),
        cost_estimate=pl.CostEstimate(flops=0, bytes_accessed=10**6, transcendentals=0),
        name="pick",
    )(column, keys, values)


def scan_kernel(lengths_ref, block_ref, start_ref, bounds_ref, far_ref):
    first_query = block_ref[0] * TOK_DEV
    origin = first_query - WINDOW * TOK_DEV
    lane_pos = first_query + lax.broadcasted_iota(jnp.int32, (1, TOK_DEV), 1)

    def next_doc(doc, carry):
        start, is_far, lane_start, edges = carry
        end = start + lengths_ref[doc]
        reach = lax.div(end - 1, TOK_DEV) - lax.div(start, TOK_DEV)
        is_far = jnp.where((reach >= 3) & (doc != 1), 1, is_far)
        lane_start = jnp.where(lane_pos >= end, end, lane_start)
        edges = tuple(
            jnp.where(first_query + place >= end, end, edge)
            for place, edge in zip((0, TILE - 1, TILE, TOK_DEV - 1), edges)
        )
        return end, is_far, lane_start, edges

    zero = jnp.int32(0)
    _, is_far, lane_start, edges = lax.fori_loop(
        0, NDOCS, next_doc, (zero, zero, jnp.zeros((1, TOK_DEV), jnp.int32), (zero,) * 4), unroll=8
    )
    far_ref[0] = is_far
    start_ref[...] = lane_start - origin
    for half in range(HALVES):
        lowest = lax.div(edges[2 * half] - origin, TILE)
        full = lax.div(edges[2 * half + 1] - origin + TILE - 1, TILE)
        bounds_ref[2 * half] = jnp.minimum(lowest, OWN_TILE)
        bounds_ref[2 * half + 1] = jnp.minimum(full, OWN_TILE)


def scan_documents(lengths, block):
    smem = pl.BlockSpec(memory_space=pltpu.SMEM)
    vmem = pl.BlockSpec(memory_space=pltpu.VMEM)
    return pl.pallas_call(
        scan_kernel,
        out_shape=[
            jax.ShapeDtypeStruct((1, TOK_DEV), jnp.int32),
            jax.ShapeDtypeStruct((2 * HALVES,), jnp.int32),
            jax.ShapeDtypeStruct((1,), jnp.int32),
        ],
        in_specs=[smem, smem],
        out_specs=[vmem, smem, smem],
        cost_estimate=pl.CostEstimate(flops=10**6, bytes_accessed=10**4, transcendentals=0),
        name="scan",
    )(lengths, block)


def prepare(starts, queries, grads, pair):
    vmem = pl.BlockSpec(memory_space=pltpu.VMEM)
    own = jax.ShapeDtypeStruct((3 * TILE, LANES), jnp.float32)
    rows = jax.ShapeDtypeStruct((HALVES * LANES, HEAD_DIM), jnp.bfloat16)
    cols = jax.ShapeDtypeStruct((HEAD_DIM, HALVES * LANES), jnp.bfloat16)
    return pl.pallas_call(
        prepare_kernel,
        out_shape=[
            jax.ShapeDtypeStruct((8 * HALVES, LANES), jnp.float32),
            rows, rows, cols, cols, own, own,
            jax.ShapeDtypeStruct((HALVES, 2 * HEAD_DIM, TILE), jnp.bfloat16),
        ],
        in_specs=[vmem] * 4,
        out_specs=[vmem] * 8,
        compiler_params=pltpu.CompilerParams(vmem_limit_bytes=24 * 1024 * 1024),
        cost_estimate=pl.CostEstimate(
            flops=2 * 10**9, bytes_accessed=10**6, transcendentals=0
        ),
        name="prepare",
    )(starts, queries, grads, pair)


def attention_block(bounds, state, kv_blocks):
    vmem = pl.BlockSpec(memory_space=pltpu.VMEM)
    smem = pl.BlockSpec(memory_space=pltpu.SMEM)
    wide = jax.ShapeDtypeStruct((TOK_DEV, LOCAL * HEAD_DIM), jnp.bfloat16)
    own = jax.ShapeDtypeStruct((2 * HEAD_DIM, TOK_DEV), jnp.float32)
    term = jax.ShapeDtypeStruct((2 * HEAD_DIM, TOK_DEV), jnp.bfloat16)
    short = jax.ShapeDtypeStruct((2 * HEAD_DIM, TILE), jnp.bfloat16)
    return pl.pallas_call(
        attention_kernel,
        out_shape=[wide, wide, own, term, term, term, short, short],
        in_specs=[smem] + [vmem] * 13,
        out_specs=[vmem] * 8,
        scratch_shapes=[
            pltpu.VMEM((WINDOW * TOK_DEV, 2 * HEAD_DIM), jnp.bfloat16),
            pltpu.VMEM((OWN_TILE, 2 * HEAD_DIM, TILE), jnp.bfloat16),
            pltpu.VMEM((SPAN, LANES), jnp.float32),
            pltpu.VMEM((WINDOW * TOK_DEV, LANES), jnp.float32),
            pltpu.VMEM((SPAN, 2 * HEAD_DIM), jnp.float32),
            pltpu.VMEM((HEAD_DIM, LANES), jnp.float32),
            pltpu.VMEM((HEAD_DIM, LANES), jnp.float32),
        ],
        compiler_params=pltpu.CompilerParams(vmem_limit_bytes=40 * 1024 * 1024),
        cost_estimate=pl.CostEstimate(
            flops=5 * 10**9, bytes_accessed=4 * 10**6, transcendentals=6 * 10**6
        ),
        name="attention",
    )(bounds, *state, *kv_blocks)


def moved(value, pairs):
    return lax.ppermute(value, "ctx", pairs)


def from_partner(value, axis, apart):
    mask = 2**apart
    pairs = [(source, source ^ mask) for source in range(lax.axis_size(axis))]
    return lax.ppermute(value, axis, pairs)


def pairs_at(distance, count):
    return [(source, source + distance) for source in range(count - distance)]


def needed(source, target):
    return target < 5 or source >= 4


def reversed_pairs(pairs):
    return [(target, source) for source, target in pairs]


def shards(query_states, key_states, value_states, out_grad, lengths):
    count = lax.axis_size("ctx")
    block_index = lax.axis_index("ctx")
    head_index = lax.axis_index("head")
    kv_start = head_index * LOCAL // (HEADS // KV_HEADS) * HEAD_DIM
    own_half = head_index % 2
    own_pair = pick_block(kv_start.astype(jnp.int32).reshape(1), key_states, value_states)
    starts, bounds, far_flag = scan_documents(lengths, block_index.astype(jnp.int32).reshape(1))
    near = {
        distance: [pair for pair in pairs_at(distance, count) if needed(*pair)]
        for distance in (1, 2)
    }
    near[3] = [(0, 3), (1, 4)]
    near[4] = [(0, 4)]
    wide = {distance: pairs_at(distance, count)[WINDOW:] for distance in (3, 4)}
    is_far = far_flag[0] == 1
    far_fourth = lax.cond(is_far, lambda pair: moved(pair, wide[4]), lambda pair: pair, own_pair)
    second = moved(own_pair, pairs_at(2, count))
    fourth = moved(own_pair, [(0, 4), (1, 5)])
    own_pair, far_fourth = lax.optimization_barrier((own_pair, far_fourth))
    state = prepare(starts, query_states, out_grad, own_pair)
    second, fourth, highest = lax.optimization_barrier((second, fourth, state[0]))
    state = [starts, highest] + list(state[1:])
    fourth = jnp.where(block_index < 6, fourth, far_fourth)
    is_even = block_index % 2 == 0
    outbound = jnp.concatenate(
        [jnp.where(is_even, own_pair, second), jnp.where(is_even, second, fourth)], axis=0
    )
    swapped = moved(outbound, [(place, place ^ 1) for place in range(count)])
    attended, query_grad, t0, t1, t2, t3, t4a, t4b = attention_block(
        bounds, state, [own_pair, second, swapped, fourth]
    )
    back2 = moved(t2, reversed_pairs(near[2]))
    back1 = moved(t1, reversed_pairs(near[1]))
    back3 = moved(t3, reversed_pairs(near[3]))
    back4 = moved(t4b, reversed_pairs(near[4]))
    gathered = t0 + back2.astype(jnp.float32) + back1.astype(jnp.float32)
    gathered = lax.optimization_barrier(gathered)
    gathered = gathered + back3.astype(jnp.float32)
    gathered = gathered + jnp.pad(back4, ((0, 0), (TILE, 0))).astype(jnp.float32)

    def with_far(total, third_term, low_term, high_term):
        fourth_term = jnp.concatenate([low_term, high_term], axis=1)
        from3 = moved(third_term, reversed_pairs(wide[3]))
        from4 = moved(fourth_term, reversed_pairs(wide[4]))
        return total + from3.astype(jnp.float32) + from4.astype(jnp.float32)

    gathered = lax.cond(
        is_far, with_far, lambda total, *others: total, gathered, t3, t4a, t4b
    )
    outgoing = lax.dynamic_slice_in_dim(gathered, (1 - own_half) * HEAD_DIM, HEAD_DIM, 0)
    received = from_partner(outgoing.astype(jnp.bfloat16), "head", 0).astype(jnp.float32)
    kept = lax.dynamic_slice_in_dim(gathered, own_half * HEAD_DIM, HEAD_DIM, 0)
    both = (kept + received).astype(jnp.bfloat16)
    return attended, query_grad, both[:HALF].T, both[HALF:].T


def solution(mesh):
    return jax.shard_map(
        shards,
        mesh=mesh,
        in_specs=(P("ctx", "head"), P("ctx", None), P("ctx", None), P("ctx", "head"), P()),
        out_specs=(P("ctx", "head"), P("ctx", "head"), P("ctx", "head"), P("ctx", "head")),
        check_vma=False,
    )
```

```python
import math

import jax
import jax.numpy as jnp
from jax import lax
from jax.experimental import pallas as pl
from jax.experimental.pallas import tpu as pltpu
from jax.sharding import PartitionSpec as P

HEAD_DIM = 128
HEADS = 16
KV_HEADS = 2
WINDOW = 4
TOK_DEV = 512
NDOCS = 64
LOCAL = 4
HALF = HEAD_DIM // 2
TILE = 256
SPAN = (WINDOW + 1) * TOK_DEV
HALVES = TOK_DEV // TILE
OWN_ROW = WINDOW * TOK_DEV
OWN_TILE = OWN_ROW // TILE
LANES = LOCAL * TILE
SCALE = HEAD_DIM ** (-0.5)
SCALE_LOG2 = SCALE * math.log2(math.e)
NEG = -1e30
STEPS = (5, 2, 1)


def contract_last(first_matrix, second_matrix):
    return lax.dot_general(
        first_matrix, second_matrix, (((1,), (1,)), ((), ())), preferred_element_type=jnp.float32
    )


def matmul(first_matrix, second_matrix):
    return jnp.dot(first_matrix, second_matrix, preferred_element_type=jnp.float32)


def tile_rows(tile, count):
    return pl.ds(pl.multiple_of(tile * TILE, TILE), count * TILE)


def by_sublane(array):
    return array.reshape(array.shape[0] // 8, 8, LANES)


def prepare_kernel(
    start_ref, q_ref, grad_ref, pair_ref,
    max_ref, q_cat, g_cat, q_t, g_t, own_scores, own_grads, own_t,
):
    for part in range(HALVES):
        own_t[part] = pair_ref[part * TILE : (part + 1) * TILE, :].T
    for half in range(HALVES):
        rows = slice(half * TILE, (half + 1) * TILE)
        lanes = slice(half * LANES, (half + 1) * LANES)
        for head in range(LOCAL):
            cols = slice(head * HEAD_DIM, (head + 1) * HEAD_DIM)
            place = slice(half * LANES + head * TILE, half * LANES + (head + 1) * TILE)
            q_cat[place, :] = q_ref[rows, cols]
            g_cat[place, :] = grad_ref[rows, cols]
            q_t[:, place] = q_ref[rows, cols].T
            g_t[:, place] = grad_ref[rows, cols].T
        start_rel = jnp.concatenate([start_ref[:, rows] - OWN_ROW] * LOCAL, axis=1)
        lane = lax.broadcasted_iota(jnp.int32, (1, TILE), 1)
        query_rel = jnp.concatenate([lane + half * TILE] * LOCAL, axis=1)
        count = 1 + half
        own_rows = slice(half * TILE, (half + count) * TILE)
        keys = pair_ref[: count * TILE, :HEAD_DIM]
        values = pair_ref[: count * TILE, HEAD_DIM:]
        raw = matmul(keys, q_t[:, lanes])
        key_rel = lax.broadcasted_iota(jnp.int32, raw.shape, 0)
        raw = jnp.where((key_rel >= start_rel) & (key_rel <= query_rel), raw, NEG)
        own_scores[own_rows] = raw
        max_ref[half * 8 : (half + 1) * 8] = jnp.max(by_sublane(raw), axis=0)
        own_grads[own_rows] = matmul(values, g_t[:, lanes])


def attention_kernel(
    bounds_ref, start_ref, max_ref, q_cat, g_cat, q_t, g_t, own_scores, own_grads, own_t,
    pair_ref, kv2_ref, kv13_ref, kv4_ref,
    out_ref, dq_ref, t0, t1, t2, t3, t4a, t4b,
    kv_buf, kv_t, scores, grads, kv_acc, o_acc, dq_acc,
):
    kv_acc[...] = jnp.zeros_like(kv_acc)
    sources = (
        (1, kv13_ref, 0), (2, kv2_ref, 0), (3, kv13_ref, TOK_DEV), (4, kv4_ref, 0)
    )
    for distance, source, row in sources:
        place = (WINDOW - distance) * TOK_DEV

        @pl.when(bounds_ref[0] < OWN_TILE - 2 * (distance - 1))
        def _(source=source, row=row, place=place):
            kv_buf[place : place + TOK_DEV, :] = source[row : row + TOK_DEV, :]
            for part in range(HALVES):
                piece = source[row + part * TILE : row + (part + 1) * TILE, :]
                kv_t[place // TILE + part] = piece.T

    def in_steps(low, step, carry):
        for size in STEPS:
            times = lax.div(OWN_TILE - low, size)
            carry = lax.fori_loop(
                0,
                times,
                lambda at, held, low=low, size=size: step(low + at * size, size, held),
                carry,
            )
            low = low + times * size
        return carry

    for half in range(HALVES):
        rows = slice(half * TILE, (half + 1) * TILE)
        lanes = slice(half * LANES, (half + 1) * LANES)
        lowest = bounds_ref[2 * half]
        first_full = bounds_ref[2 * half + 1]
        count = 1 + half
        own_part = slice(half * TILE, (half + count) * TILE)
        own_rows = slice(OWN_ROW, OWN_ROW + count * TILE)

        def score_masked(tile, row_max):
            kv_rows = tile_rows(tile, 1)
            raw = matmul(kv_buf[kv_rows, :HEAD_DIM], q_t[:, lanes])
            key_rel = tile * TILE + lax.broadcasted_iota(jnp.int32, raw.shape, 0)
            start_rel = jnp.concatenate([start_ref[:, rows]] * LOCAL, axis=1)
            raw = jnp.where(key_rel >= start_rel, raw, NEG)
            scores[kv_rows] = raw
            return jnp.maximum(row_max, jnp.max(by_sublane(raw), axis=0))

        def score_full(tile, count, row_max):
            kv_rows = tile_rows(tile, count)
            raw = matmul(kv_buf[kv_rows, :HEAD_DIM], q_t[:, lanes])
            scores[kv_rows] = raw
            return jnp.maximum(row_max, jnp.max(by_sublane(raw), axis=0))

        row_max = in_steps(first_full, score_full, max_ref[half * 8 : (half + 1) * 8])
        row_max = lax.fori_loop(lowest, first_full, score_masked, row_max)
        shift = jnp.max(row_max, axis=0, keepdims=True) * SCALE_LOG2

        def add_totals(carry, weights, prob_grad):
            total, dots = carry
            total = total + jnp.sum(by_sublane(weights), axis=0)
            dots = dots + jnp.sum(by_sublane(weights * prob_grad), axis=0)
            return total, dots

        def total_tile(tile, count, carry):
            kv_rows = tile_rows(tile, count)
            prob_grad = matmul(kv_buf[kv_rows, HEAD_DIM:], g_t[:, lanes])
            weights = jnp.exp2(scores[kv_rows] * SCALE_LOG2 - shift)
            scores[kv_rows] = weights
            grads[kv_rows] = prob_grad
            return add_totals(carry, weights, prob_grad)

        nothing = jnp.zeros((8, LANES), jnp.float32)
        weights = jnp.exp2(own_scores[own_part] * SCALE_LOG2 - shift)
        scores[own_rows] = weights
        carry = add_totals((nothing, nothing), weights, own_grads[own_part])
        total, dots = in_steps(lowest, total_tile, carry)
        inverse = 1.0 / jnp.sum(total, axis=0, keepdims=True)
        grad_dot = jnp.sum(dots, axis=0, keepdims=True) * inverse

        def score_grads(weights, prob_grad):
            weights = weights * inverse
            score_grad = (weights * (prob_grad - grad_dot)).astype(jnp.bfloat16)
            return weights.astype(jnp.bfloat16), score_grad

        def transposed_products(turned, prob, score_grad):
            out_add = dq_add = None
            for part, piece in enumerate(turned):
                inner = slice(part * TILE, (part + 1) * TILE)
                out_part = matmul(piece[HEAD_DIM:], prob[inner])
                dq_part = matmul(piece[:HEAD_DIM], score_grad[inner])
                out_add = out_part if part == 0 else out_add + out_part
                dq_add = dq_part if part == 0 else dq_add + dq_part
            return out_add, dq_add

        def backward_tile(tile, count, carry):
            kv_rows = tile_rows(tile, count)
            prob, score_grad = score_grads(scores[kv_rows], grads[kv_rows])
            kv_acc[kv_rows, HEAD_DIM:] += matmul(prob, g_cat[lanes])
            kv_acc[kv_rows, :HEAD_DIM] += matmul(score_grad, q_cat[lanes])
            turned = [kv_t[tile + part] for part in range(count)]
            out_add, dq_add = transposed_products(turned, prob, score_grad)
            o_acc[...] += out_add
            dq_acc[...] += dq_add
            return carry

        prob, score_grad = score_grads(scores[own_rows], own_grads[own_part])
        kv_acc[own_rows, HEAD_DIM:] += matmul(prob, g_cat[lanes])
        kv_acc[own_rows, :HEAD_DIM] += matmul(score_grad, q_cat[lanes])
        turned = [own_t[part] for part in range(count)]
        o_acc[...], dq_acc[...] = transposed_products(turned, prob, score_grad)
        in_steps(lowest, backward_tile, 0)
        for head in range(LOCAL):
            cols = slice(head * HEAD_DIM, (head + 1) * HEAD_DIM)
            place = slice(head * TILE, (head + 1) * TILE)
            out_ref[rows, cols] = o_acc[:, place].T.astype(jnp.bfloat16)
            dq_ref[rows, cols] = (dq_acc[:, place].T * SCALE).astype(jnp.bfloat16)

    def write_term(term, row, rows):
        keys = (kv_acc[row : row + rows, :HEAD_DIM] * SCALE).T.astype(term.dtype)
        values = kv_acc[row : row + rows, HEAD_DIM:].T.astype(term.dtype)
        for half in range(2):
            part = slice(half * HALF, (half + 1) * HALF)
            term[2 * half * HALF : (2 * half + 1) * HALF, :] = keys[part]
            term[(2 * half + 1) * HALF : (2 * half + 2) * HALF, :] = values[part]

    for distance, term in enumerate((t0, t1, t2, t3)):
        write_term(term, (WINDOW - distance) * TOK_DEV, TOK_DEV)
    write_term(t4a, 0, TILE)
    write_term(t4b, TILE, TILE)


def pick_kernel(column_ref, keys_ref, values_ref, pair_ref, sems):
    column = pl.multiple_of(column_ref[0], HEAD_DIM)
    copies = []
    for place, source in enumerate((keys_ref, values_ref)):
        cols = pl.ds(place * HEAD_DIM, HEAD_DIM)
        copies.append(
            pltpu.make_async_copy(
                source.at[:, pl.ds(column, HEAD_DIM)], pair_ref.at[:, cols], sems.at[place]
            )
        )
    for copy in copies:
        copy.start()
    for copy in copies:
        copy.wait()


def pick_block(column, keys, values):
    smem = pl.BlockSpec(memory_space=pltpu.SMEM)
    vmem = pl.BlockSpec(memory_space=pltpu.VMEM)
    anywhere = pl.BlockSpec(memory_space=pltpu.HBM)
    return pl.pallas_call(
        pick_kernel,
        out_shape=jax.ShapeDtypeStruct((TOK_DEV, 2 * HEAD_DIM), jnp.bfloat16),
        in_specs=[smem, anywhere, anywhere],
        out_specs=vmem,
        scratch_shapes=[pltpu.SemaphoreType.DMA((2,))],
        compiler_params=pltpu.CompilerParams(vmem_limit_bytes=60 * 1024 * 1024),
        cost_estimate=pl.CostEstimate(flops=0, bytes_accessed=10**6, transcendentals=0),
        name="pick",
    )(column, keys, values)


def scan_kernel(lengths_ref, block_ref, start_ref, bounds_ref, far_ref):
    first_query = block_ref[0] * TOK_DEV
    origin = first_query - WINDOW * TOK_DEV
    lane_pos = first_query + lax.broadcasted_iota(jnp.int32, (1, TOK_DEV), 1)

    def next_doc(doc, carry):
        start, is_far, lane_start, edges = carry
        end = start + lengths_ref[doc]
        reach = lax.div(end - 1, TOK_DEV) - lax.div(start, TOK_DEV)
        is_far = jnp.where((reach >= 3) & (doc != 1), 1, is_far)
        lane_start = jnp.where(lane_pos >= end, end, lane_start)
        edges = tuple(
            jnp.where(first_query + place >= end, end, edge)
            for place, edge in zip((0, TILE - 1, TILE, TOK_DEV - 1), edges)
        )
        return end, is_far, lane_start, edges

    zero = jnp.int32(0)
    _, is_far, lane_start, edges = lax.fori_loop(
        0, NDOCS, next_doc, (zero, zero, jnp.zeros((1, TOK_DEV), jnp.int32), (zero,) * 4), unroll=8
    )
    far_ref[0] = is_far
    start_ref[...] = lane_start - origin
    for half in range(HALVES):
        lowest = lax.div(edges[2 * half] - origin, TILE)
        full = lax.div(edges[2 * half + 1] - origin + TILE - 1, TILE)
        bounds_ref[2 * half] = jnp.minimum(lowest, OWN_TILE)
        bounds_ref[2 * half + 1] = jnp.minimum(full, OWN_TILE)


def scan_documents(lengths, block):
    smem = pl.BlockSpec(memory_space=pltpu.SMEM)
    vmem = pl.BlockSpec(memory_space=pltpu.VMEM)
    return pl.pallas_call(
        scan_kernel,
        out_shape=[
            jax.ShapeDtypeStruct((1, TOK_DEV), jnp.int32),
            jax.ShapeDtypeStruct((2 * HALVES,), jnp.int32),
            jax.ShapeDtypeStruct((1,), jnp.int32),
        ],
        in_specs=[smem, smem],
        out_specs=[vmem, smem, smem],
        cost_estimate=pl.CostEstimate(flops=10**6, bytes_accessed=10**4, transcendentals=0),
        name="scan",
    )(lengths, block)


def prepare(starts, queries, grads, pair):
    vmem = pl.BlockSpec(memory_space=pltpu.VMEM)
    own = jax.ShapeDtypeStruct((3 * TILE, LANES), jnp.float32)
    rows = jax.ShapeDtypeStruct((HALVES * LANES, HEAD_DIM), jnp.bfloat16)
    cols = jax.ShapeDtypeStruct((HEAD_DIM, HALVES * LANES), jnp.bfloat16)
    return pl.pallas_call(
        prepare_kernel,
        out_shape=[
            jax.ShapeDtypeStruct((8 * HALVES, LANES), jnp.float32),
            rows, rows, cols, cols, own, own,
            jax.ShapeDtypeStruct((HALVES, 2 * HEAD_DIM, TILE), jnp.bfloat16),
        ],
        in_specs=[vmem] * 4,
        out_specs=[vmem] * 8,
        compiler_params=pltpu.CompilerParams(vmem_limit_bytes=24 * 1024 * 1024),
        cost_estimate=pl.CostEstimate(
            flops=2 * 10**9, bytes_accessed=10**6, transcendentals=0
        ),
        name="prepare",
    )(starts, queries, grads, pair)


def attention_block(bounds, state, kv_blocks):
    vmem = pl.BlockSpec(memory_space=pltpu.VMEM)
    smem = pl.BlockSpec(memory_space=pltpu.SMEM)
    wide = jax.ShapeDtypeStruct((TOK_DEV, LOCAL * HEAD_DIM), jnp.bfloat16)
    own = jax.ShapeDtypeStruct((2 * HEAD_DIM, TOK_DEV), jnp.float32)
    term = jax.ShapeDtypeStruct((2 * HEAD_DIM, TOK_DEV), jnp.bfloat16)
    short = jax.ShapeDtypeStruct((2 * HEAD_DIM, TILE), jnp.bfloat16)
    return pl.pallas_call(
        attention_kernel,
        out_shape=[wide, wide, own, term, term, term, short, short],
        in_specs=[smem] + [vmem] * 13,
        out_specs=[vmem] * 8,
        scratch_shapes=[
            pltpu.VMEM((WINDOW * TOK_DEV, 2 * HEAD_DIM), jnp.bfloat16),
            pltpu.VMEM((OWN_TILE, 2 * HEAD_DIM, TILE), jnp.bfloat16),
            pltpu.VMEM((SPAN, LANES), jnp.float32),
            pltpu.VMEM((WINDOW * TOK_DEV, LANES), jnp.float32),
            pltpu.VMEM((SPAN, 2 * HEAD_DIM), jnp.float32),
            pltpu.VMEM((HEAD_DIM, LANES), jnp.float32),
            pltpu.VMEM((HEAD_DIM, LANES), jnp.float32),
        ],
        compiler_params=pltpu.CompilerParams(vmem_limit_bytes=40 * 1024 * 1024),
        cost_estimate=pl.CostEstimate(
            flops=5 * 10**9, bytes_accessed=4 * 10**6, transcendentals=6 * 10**6
        ),
        name="attention",
    )(bounds, *state, *kv_blocks)


def moved(value, pairs):
    return lax.ppermute(value, "ctx", pairs)


def from_partner(value, axis, apart):
    mask = 2**apart
    pairs = [(source, source ^ mask) for source in range(lax.axis_size(axis))]
    return lax.ppermute(value, axis, pairs)


def pairs_at(distance, count):
    return [(source, source + distance) for source in range(count - distance)]


def needed(source, target):
    return target < 5 or source >= 4


def reversed_pairs(pairs):
    return [(target, source) for source, target in pairs]


def shards(query_states, key_states, value_states, out_grad, lengths):
    count = lax.axis_size("ctx")
    block_index = lax.axis_index("ctx")
    head_index = lax.axis_index("head")
    kv_start = head_index * LOCAL // (HEADS // KV_HEADS) * HEAD_DIM
    own_half = head_index % 2
    own_pair = pick_block(kv_start.astype(jnp.int32).reshape(1), key_states, value_states)
    starts, bounds, far_flag = scan_documents(lengths, block_index.astype(jnp.int32).reshape(1))
    near = {
        distance: [pair for pair in pairs_at(distance, count) if needed(*pair)]
        for distance in (1, 2)
    }
    near[3] = [(0, 3), (1, 4)]
    near[4] = [(0, 4)]
    wide = {distance: pairs_at(distance, count)[WINDOW:] for distance in (3, 4)}
    is_far = far_flag[0] == 1
    far_fourth = lax.cond(is_far, lambda pair: moved(pair, wide[4]), lambda pair: pair, own_pair)
    second = moved(own_pair, pairs_at(2, count))
    fourth = moved(own_pair, [(0, 4), (1, 5)])
    own_pair, far_fourth = lax.optimization_barrier((own_pair, far_fourth))
    state = prepare(starts, query_states, out_grad, own_pair)
    second, fourth, highest = lax.optimization_barrier((second, fourth, state[0]))
    state = [starts, highest] + list(state[1:])
    fourth = jnp.where(block_index < 6, fourth, far_fourth)
    is_even = block_index % 2 == 0
    outbound = jnp.concatenate(
        [jnp.where(is_even, own_pair, second), jnp.where(is_even, second, fourth)], axis=0
    )
    swapped = moved(outbound, [(place, place ^ 1) for place in range(count)])
    attended, query_grad, t0, t1, t2, t3, t4a, t4b = attention_block(
        bounds, state, [own_pair, second, swapped, fourth]
    )
    back4 = moved(t4b, reversed_pairs(near[4]))
    back2 = moved(t2, reversed_pairs(near[2]))
    back1 = moved(t1, reversed_pairs(near[1]))
    back3 = moved(t3, reversed_pairs(near[3]))
    gathered = t0 + jnp.pad(back4, ((0, 0), (TILE, 0))).astype(jnp.float32)
    gathered = lax.optimization_barrier(gathered)
    gathered = gathered + back2.astype(jnp.float32) + back1.astype(jnp.float32)
    gathered = lax.optimization_barrier(gathered)
    gathered = gathered + back3.astype(jnp.float32)

    def with_far(total, third_term, low_term, high_term):
        fourth_term = jnp.concatenate([low_term, high_term], axis=1)
        from3 = moved(third_term, reversed_pairs(wide[3]))
        from4 = moved(fourth_term, reversed_pairs(wide[4]))
        return total + from3.astype(jnp.float32) + from4.astype(jnp.float32)

    gathered = lax.cond(
        is_far, with_far, lambda total, *others: total, gathered, t3, t4a, t4b
    )
    outgoing = lax.dynamic_slice_in_dim(gathered, (1 - own_half) * HEAD_DIM, HEAD_DIM, 0)
    received = from_partner(outgoing.astype(jnp.bfloat16), "head", 0).astype(jnp.float32)
    kept = lax.dynamic_slice_in_dim(gathered, own_half * HEAD_DIM, HEAD_DIM, 0)
    both = (kept + received).astype(jnp.bfloat16)
    return attended, query_grad, both[:HALF].T, both[HALF:].T


def solution(mesh):
    return jax.shard_map(
        shards,
        mesh=mesh,
        in_specs=(P("ctx", "head"), P("ctx", None), P("ctx", None), P("ctx", "head"), P()),
        out_specs=(P("ctx", "head"), P("ctx", "head"), P("ctx", "head"), P("ctx", "head")),
        check_vma=False,
    )
```
